256 devices in a mesh: tm: 16 (over z, core), gx: 4 (over y), gy: 4 (over x).
Axes of the slice: x: 4, y: 4, z: 8, core: 2. Of those that a mesh axis runs over, the one named last changes fastest.
Arguments:
- field: float32 [16, 32, 32, 256], P('tm', 'gx', 'gy'), may hold values from -6 to 6
- modes: float32 [16, 16, 32, 32, 256], P('tm', None, 'gx', 'gy'), may hold values from -2 to 2
- source: float32 [32, 32, 256], P('gx', 'gy'), may hold values from -6 to 6
- regions: int32 [32, 32, 256], P('gx', 'gy'), may hold values from 0 to 7
- region_kappa: float32 [8], replicated, may hold values from 0.6 to 1
- mode_rate: float32 [16], replicated, may hold values from 0.02 to 4
- mode_weight: float32 [16], replicated, may hold values from 0.02 to 0.3
Outputs:
- new_field: float32 [16, 32, 32, 256], P('tm', 'gx', 'gy')
- new_modes: float32 [16, 16, 32, 32, 256], P('tm', None, 'gx', 'gy')
- correction_size: float32 [16], P('tm')
The draws below stay inside these ranges and needn't reach their ends.
All inputs are finite; a program needn't handle non-finite values.
Results may differ from the reference program's by a relative error of at most 0.00021.
Values sent between devices are 32-bit elements; how exact they have to be, the bound alone decides.
No kernel may reach another device: no remote copies, remote signals or barrier semaphores. Data moves between devices by JAX's collectives and lax.ppermute only.
A program may use at most 64 MiB of HBM per device.

```python
import math
import jax
import jax.numpy as jnp
from jax import lax

CZ = 256
MODES = 16
SUBSTEPS = 2
NREG = 8
NX = 32
NY = 32
N_TM = 16


def set_ends(drawn, stream_key, low, largest):
    dims = drawn.shape
    place = [jax.random.randint(jax.random.fold_in(stream_key, axis), (), 0, dims[axis]) for axis in range(len(dims))]
    drawn = drawn.at[tuple(place)].set(low)
    longest = dims.index(max(dims))
    place[longest] = (place[longest] + 1) % dims[longest]
    return drawn.at[tuple(place)].set(largest)


def block_scale(rng, extent, pieces, low, high):
    level, own = 1.0, jax.random.fold_in(rng, 6)
    for axis_at, blocks in pieces:
        heights = jnp.exp(jax.random.uniform(jax.random.fold_in(own, axis_at), (blocks,), jnp.float32, low / len(pieces), high / len(pieces)))
        level = level * jnp.repeat(heights, extent[axis_at] // blocks).reshape([-1 if axis == axis_at else 1 for axis in range(len(extent))])
    return level


def gaussian(rng, extent, spread, reach, pieces=(), kind=jnp.bfloat16):
    values = jax.random.normal(rng, extent, jnp.float32) * spread
    if len(pieces) > 0:
        values = block_scale(rng, extent, pieces, -0.22, 0.18) * values
    return jnp.clip(values, min=-reach, max=reach).astype(kind)


def setup_inputs(seed: int = 0) -> dict:
    splits = jax.random.split(jax.random.key(seed), 8)
    field = gaussian(splits[0], (N_TM, NX, NY, CZ), 1.0, 6.0, ((0, 16), (1, 4), (2, 4)), jnp.float32)
    modes = gaussian(splits[1], (N_TM, MODES, NX, NY, CZ), 0.3, 2.0, ((0, 16), (2, 4), (3, 4)), jnp.float32)
    source = gaussian(splits[2], (NX, NY, CZ), 1.0, 6.0, ((0, 4), (1, 4)), jnp.float32)
    regions = set_ends(jax.random.randint(splits[3], (NX, NY, CZ), 0, NREG), jax.random.fold_in(splits[3], 1), 0, NREG - 1).astype(jnp.int32)
    region_kappa = jnp.clip(jnp.exp(jax.random.uniform(splits[4], (NREG,), jnp.float32, math.log(0.6), math.log(1.0))), 0.6, 1.0)
    mode_rate = jnp.clip(jnp.exp(jax.random.uniform(splits[5], (MODES,), jnp.float32, math.log(0.02), math.log(4.0))), 0.02, 4.0)
    mode_weight = jnp.clip(jnp.exp(jax.random.uniform(splits[6], (MODES,), jnp.float32, math.log(0.02), math.log(0.3))), 0.02, 0.3)
    return {"field": field, "modes": modes, "source": source, "regions": regions, "region_kappa": region_kappa, "mode_rate": mode_rate, "mode_weight": mode_weight}


coarse_size = 0.12

def laplace(padded_field, padded_kappa):
    centre_field = padded_field[1:-1, 1:-1, 1:-1]
    centre_kappa = padded_kappa[1:-1, 1:-1, 1:-1]
    total = jnp.zeros_like(centre_field)
    offsets = [(2, 1, 1), (0, 1, 1), (1, 2, 1), (1, 0, 1), (1, 1, 2), (1, 1, 0)]
    sx, sy, sz = centre_field.shape
    for ox, oy, oz in offsets:
        near_field = padded_field[ox:ox + sx, oy:oy + sy, oz:oz + sz]
        near_kappa = padded_kappa[ox:ox + sx, oy:oy + sy, oz:oz + sz]
        total = total + 0.5 * (centre_kappa + near_kappa) * (near_field - centre_field)
    return total

def advance(field, modes, padded_field, padded_kappa, source, step_size, decay, mode_weight):
    memory = jnp.einsum('m,mxyz->xyz', mode_weight, modes, precision=lax.Precision.HIGHEST)
    change = step_size * (laplace(padded_field, padded_kappa) - memory + source)
    new_modes = decay[:, None, None, None] * modes + (1.0 - decay)[:, None, None, None] * change[None]
    return (field + change, new_modes)

def cell_kappa(regions, region_kappa):
    table = jnp.arange(region_kappa.shape[0], dtype=jnp.int32)
    onehot = regions[..., None] == table
    return lax.optimization_barrier(jnp.sum(jnp.where(onehot, region_kappa, jnp.float32(0.0)), axis=-1))

def reference(field, modes, source, regions, region_kappa, mode_rate, mode_weight):
    padded_kappa = jnp.pad(cell_kappa(regions, region_kappa), 1)
    coarse_decay = jnp.exp(-mode_rate)
    fine_decay = jnp.exp(-mode_rate / SUBSTEPS)

    def coarse(u, h):
        return advance(u, h, jnp.pad(u, 1), padded_kappa, source, coarse_size, coarse_decay, mode_weight)

    def fine(u, h):
        for turn in range(SUBSTEPS):
            u, h = advance(u, h, jnp.pad(u, 1), padded_kappa, source, coarse_size / SUBSTEPS, fine_decay, mode_weight)
        return (u, h)
    walk_u, walk_h = (field[0], modes[0])
    out_u, out_h, sizes = ([], [], [])
    for slot in range(N_TM):
        fine_u, fine_h = fine(field[slot], modes[slot])
        old_u, old_h = coarse(field[slot], modes[slot])
        now_u, now_h = coarse(walk_u, walk_h)
        walk_u = now_u + fine_u - old_u
        walk_h = now_h + fine_h - old_h
        out_u.append(walk_u)
        out_h.append(walk_h)
        diff = walk_u - fine_u
        sizes.append(jnp.sqrt(jnp.sum(diff * diff) / (NX * NY * CZ)))
    return (jnp.stack(out_u), jnp.stack(out_h), jnp.stack(sizes))
```

```python
import functools
import jax
import jax.numpy as jnp
from jax import lax
from jax.experimental import pallas as pl
from jax.experimental.pallas import tpu as pltpu
from jax.sharding import PartitionSpec as P

STEP = 0.12
F32 = jnp.float32
VM = pl.BlockSpec(memory_space=pltpu.VMEM)
SM = pl.BlockSpec(memory_space=pltpu.SMEM)
PARAMS = pltpu.CompilerParams(vmem_limit_bytes=40 * 1024 * 1024)
HALO = 15
TRI = [HALO] + [HALO - j for j in range(1, HALO)]
OFF = [sum(TRI[:j]) for j in range(HALO)]
KOFF = sum(TRI)
MSG = KOFF + HALO
LAY = 48
NEW = 46


def call(kernel, outs, ins, smem, scratch=()):
    return pl.pallas_call(
        kernel,
        out_shape=[jax.ShapeDtypeStruct(shape, F32) for shape in outs],
        in_specs=[SM] * smem + [VM] * (ins - smem),
        out_specs=[VM] * len(outs),
        scratch_shapes=[pltpu.VMEM(shape, F32) for shape in scratch],
        compiler_params=PARAMS,
    )


def lane_low(shape):
    return lax.broadcasted_iota(jnp.int32, shape, len(shape) - 1) < 64


def local_kernel(rk, w, wf, u, reg, s, modes, kap, g0, q1s, up, dn):
    for x in range(8):
        rows = slice(8 * x, 8 * x + 8)
        region = reg[rows]
        k = jnp.zeros((8, 256), F32)
        for r in range(8):
            k = jnp.where(region == r, rk[r], k)
        kap[rows] = k
        a = jnp.zeros((8, 256), F32)
        b = jnp.zeros((8, 256), F32)
        for m in range(16):
            h = modes[m, rows]
            a += w[m] * h
            b += wf[m] * h
        g0[rows] = s[rows] - a
        q1s[rows] = s[rows] - b
    up[0:16] = u[48:64]
    up[16:32] = kap[48:64]
    up[32:40] = g0[56:64]
    dn[0:16] = u[0:16]
    dn[16:32] = kap[0:16]
    dn[32:40] = g0[0:8]


def scatter_pack_kernel(at, u, s, kap, modes, sk, packed):
    sk[...] = jnp.concatenate([s[...], kap[...]], axis=0).T

    @pl.when(at[0] == 0)
    def _():
        for m in range(8):
            both = jnp.concatenate([modes[m], modes[m + 8]], axis=0).T
            packed[:, 16 * m : 16 * m + 16] = both.reshape(16, 16, 128)
        both = jnp.concatenate([u[...], u[...]], axis=0).T
        packed[:, 128:144] = both.reshape(16, 16, 128)


def side_kernel(at, u, kap, g0, xlo, xhi, yup, ydn):
    has_lo = jnp.where(at[1] > 0, 1.0, 0.0).astype(F32)
    has_hi = jnp.where(at[1] < 3, 1.0, 0.0).astype(F32)
    for out, first in ((yup, 6), (ydn, 0)):
        for piece in range(5):
            if piece < 4:
                src, base = (u, 0) if piece < 2 else (kap, 16)
                y = first + piece % 2
                out[16 * piece : 16 * piece + 1] = has_lo * xlo[base + 8 + y : base + 9 + y]
                out[16 * piece + 9 : 16 * piece + 10] = has_hi * xhi[base + y : base + y + 1]
            else:
                src = g0
                y = 7 if first else 0
            for x in range(8):
                at_row = 16 * piece + 1 + x
                out[at_row : at_row + 1] = src[8 * x + y : 8 * x + y + 1]


def fine_kernel(at, omega, u, kap, g0, q1s, xlo, xhi, ylo, yhi, fine, both, up, kp, gp, u1):
    gx, gy = at[1], at[2]
    zero = jnp.zeros((24, 256), F32)
    for ref in (up, kp, gp):
        for x in range(12):
            ref[x] = zero
    for x in range(8):
        rows = slice(8 * x, 8 * x + 8)
        up[2 + x, 8:16] = u[rows]
        kp[2 + x, 8:16] = kap[rows]
        gp[2 + x, 8:16] = g0[rows]

    @pl.when(gx > 0)
    def _():
        for i in range(2):
            up[i, 8:16] = xlo[8 * i : 8 * i + 8]
            kp[i, 8:16] = xlo[16 + 8 * i : 24 + 8 * i]
        gp[1, 8:16] = xlo[32:40]

    @pl.when(gx < 3)
    def _():
        for i in range(2):
            up[10 + i, 8:16] = xhi[8 * i : 8 * i + 8]
            kp[10 + i, 8:16] = xhi[16 + 8 * i : 24 + 8 * i]
        gp[10, 8:16] = xhi[32:40]

    for cond, ref, row in ((gy > 0, ylo, 6), (gy < 3, yhi, 16)):

        @pl.when(cond)
        def _(ref=ref, row=row):
            for x in range(10):
                for i in range(2):
                    up[1 + x, row + i : row + i + 1] = ref[16 * i + x : 16 * i + x + 1]
                    kp[1 + x, row + i : row + i + 1] = ref[32 + 16 * i + x : 33 + 16 * i + x]
                if 1 <= x <= 8:
                    near = 7 if row == 6 else 16
                    gp[1 + x, near : near + 1] = ref[64 + x : 65 + x]

    z = lax.broadcasted_iota(jnp.int32, (24, 256), 1)

    def above(v):
        return jnp.where(z == 255, 0.0, pltpu.roll(v, 255, 1))

    def below(v):
        return jnp.where(z == 0, 0.0, pltpu.roll(v, 1, 1))

    def laplace(ref, x):
        uc, kc = ref[x], kp[x]
        total = jnp.zeros((24, 256), F32)
        for near_u, near_k in (
            (ref[x + 1], kp[x + 1]),
            (ref[x - 1], kp[x - 1]),
            (pltpu.roll(uc, 23, 0), pltpu.roll(kc, 23, 0)),
            (pltpu.roll(uc, 1, 0), pltpu.roll(kc, 1, 0)),
            (above(uc), above(kc)),
            (below(uc), below(kc)),
        ):
            total += (kc + near_k) * (near_u - uc)
        return 0.5 * total

    for x in range(1, 11):
        change = (0.5 * STEP) * (laplace(up, x) + gp[x])
        u1[x] = up[x] + change
        gp[x] = change

    @pl.when(gx == 0)
    def _():
        u1[1] = zero

    @pl.when(gx == 3)
    def _():
        u1[10] = zero

    @pl.when(gy == 0)
    def _():
        for x in range(1, 11):
            u1[x, 0:8] = zero[0:8]

    @pl.when(gy == 3)
    def _():
        for x in range(1, 11):
            u1[x, 16:24] = zero[0:8]

    first, second = [], []
    for x in range(8):
        rows = slice(8 * x, 8 * x + 8)
        c1 = gp[2 + x, 8:16]
        lap = laplace(u1, 2 + x)[8:16]
        c2 = (0.5 * STEP) * (lap + q1s[rows] - omega[0] * c1)
        fine[rows] = u1[2 + x, 8:16] + c2
        first.append(c1)
        second.append(c2)
    both[...] = jnp.concatenate(first + second, axis=0).T


def doubled(v, low):
    turned = pltpu.roll(v, 64, 1)
    return jnp.where(low, v, turned), jnp.where(low, turned, v)


def known_kernel(at, parts, sk, start, coef, msg, known):
    low = lane_low((16, 128))
    slab = sk[pl.ds(pl.multiple_of(at[0] * 16, 16), 16), :]
    source, kap = doubled(slab, low)
    h = [start[16 * m : 16 * m + 16] for m in range(8)]
    field = start[128:144]
    seen = []
    for j in range(16):
        c1, c2 = doubled(parts[j], low)
        if j == 0:
            n = 2.0 * c1
            seen.append(field + c1 + c2)
        else:
            q = coef[24:25] * h[0]
            for m in range(1, 8):
                q += coef[24 + m : 25 + m] * h[m]
            n = STEP * (source - (q + pltpu.roll(q, 64, 1)))
            seen.append(n + c2 - c1)
        known[j] = n
        xn = c2 - 2.0 * c1 + n
        yn = n - c1
        for m in range(8):
            h[m] = coef[m : m + 1] * h[m] + coef[16 + m : 17 + m] * (xn + coef[8 + m : 9 + m] * yn)
    rows = [jnp.where(low, seen[j], seen[j + 8]) for j in range(8)]
    last = jnp.where(low[0:8], kap[0:8], kap[8:16])
    for p in range(16):
        for j in range(8):
            msg[p, 16 * j : 16 * j + 16] = rows[j]
        msg[p, 128:136] = last


def gather_kernel(got, own, kap, up, dn):
    low = lane_low((8, 128))

    def pair(row):
        even = got[pl.ds(row, 8, stride=272), :]
        odd = got[pl.ds(row + 136, 8, stride=272), :]
        left = jnp.where(low, even, pltpu.roll(odd, 64, 1))
        right = jnp.where(low, pltpu.roll(even, 64, 1), odd)
        return left, right

    def place(j, z, v):
        own[j, z] = v
        if j < HALO:
            if z < TRI[j]:
                dn[OFF[j] + z] = v
            if z >= 16 - TRI[j]:
                up[OFF[j] + z - (16 - TRI[j])] = v

    for j in range(8):
        for z in range(16):
            left, right = pair(16 * j + z)
            place(j, z, left)
            place(j + 8, z, right)
    for z in range(8):
        left, right = pair(128 + z)
        for at, v in ((z, left), (z + 8, right)):
            kap[at] = v
            if at < HALO:
                dn[KOFF + at] = v
            if at >= 1:
                up[KOFF + at - 1] = v


def sweep_kernel(at, beta, own, kown, lo, hi, parts, known, start, coef, out, v, e, g, c, kw):
    t = at[0]
    p = at[1] * 4 + at[2]
    has_lo = jnp.where(t > 0, 1.0, 0.0).astype(F32)
    has_hi = jnp.where(t < 15, 1.0, 0.0).astype(F32)

    def row(j, layer):
        return pl.ds(pl.multiple_of((j * LAY + layer) * 8, 8), 8)

    zero = jnp.zeros((8, 128), F32)
    for j in range(16):
        dst = e if j == 0 else v
        if j < HALO:
            n = TRI[j]
            for i in range(n):
                dst[row(j, HALO - n + i), :] = has_lo * lo[OFF[j] + i]
                dst[row(j, 31 + i), :] = has_hi * hi[OFF[j] + i]
        for i in range(16):
            dst[row(j, 15 + i), :] = own[j, i]
    kw[0] = zero
    kw[47] = zero
    for i in range(HALO):
        kw[1 + i] = has_lo * lo[KOFF + i]
        kw[32 + i] = has_hi * hi[KOFF + i]
    for i in range(16):
        kw[16 + i] = kown[i]

    lane = lax.broadcasted_iota(jnp.int32, (8, 128), 1)
    sub = lax.broadcasted_iota(jnp.int32, (8, 128), 0)
    y, x, half = lane % 8, (lane // 8) % 8, lane // 64
    half_y, gx = sub % 2, sub // 2
    y_end, y_start = y == 7, y == 0
    x_end, x_start = x == 7, x == 0
    turn_up, turn_dn = half == 1, half == 0
    inside = (
        jnp.logical_not(x_end & (gx == 3)),
        jnp.logical_not(x_start & (gx == 0)),
        jnp.logical_not(y_end & (half == 1) & (half_y == 1)),
        jnp.logical_not(y_start & (half == 0) & (half_y == 0)),
    )

    def near(a):
        far = pltpu.roll(a, 56, 1)
        xp = jnp.where(x_end, pltpu.roll(far, 6, 0), pltpu.roll(a, 120, 1))
        far = pltpu.roll(a, 72, 1)
        xm = jnp.where(x_start, pltpu.roll(far, 2, 0), pltpu.roll(a, 8, 1))
        far = pltpu.roll(a, 71, 1)
        far = jnp.where(turn_up, pltpu.roll(far, 7, 0), far)
        yp = jnp.where(y_end, far, pltpu.roll(a, 127, 1))
        far = pltpu.roll(a, 57, 1)
        far = jnp.where(turn_dn, pltpu.roll(far, 1, 0), far)
        ym = jnp.where(y_start, far, pltpu.roll(a, 1, 1))
        return xp, xm, yp, ym

    def faces(layer, carry):
        kc = kw[layer + 1]
        place = t * 16 - HALO + layer
        scale = jnp.where((place >= 0) & (place < 256), 0.5 * STEP, 0.0).astype(F32)
        total = zero
        for i, kn in enumerate(near(kc)):
            face = scale * (kc + jnp.where(inside[i], kn, 0.0))
            total += face
            c[i, layer] = jnp.where(inside[i], face, 0.0)
        for i, kn in ((4, kw[layer + 2]), (5, kw[layer])):
            face = scale * (kc + kn)
            total += face
            c[i, layer] = face
        c[6, layer] = -total
        return carry

    lax.fori_loop(0, NEW, faces, 0)

    for j in range(1, 16):
        count = NEW - 2 * j
        block = 4 if count % 4 == 0 else 2

        def layers(i, carry, j=j, block=block):
            for k in range(block):
                layer = j + i * block + k
                mid = e[row(j - 1, layer), :]
                acc = c[6, layer] * mid
                acc += c[4, layer] * e[row(j - 1, layer + 1), :]
                acc += c[5, layer] * e[row(j - 1, layer - 1), :]
                for d, un in enumerate(near(mid)):
                    acc += c[d, layer] * un
                for i2 in range(1, j):
                    acc -= beta[j - 1 - i2] * g[row(i2 - 1, layer), :]
                g[row(j - 1, layer), :] = acc
                e[row(j, layer), :] = mid + acc + v[row(j, layer), :]
            return carry

        lax.fori_loop(0, count // block, layers, 0)

    low = lane_low((16, 128))
    sublane = p // 2
    mine = low == (p % 2 == 0)

    def block_of(ref, j):
        first = (j * LAY + HALO) * 8 + sublane
        a = ref[pl.ds(first, 8, stride=8), :]
        b = ref[pl.ds(first + 64, 8, stride=8), :]
        got = jnp.concatenate([a, b], axis=0)
        return jnp.where(mine, got, pltpu.roll(got, 64, 1))

    h = [start[16 * m : 16 * m + 16] for m in range(8)]
    for j in range(16):
        c1, c2 = doubled(parts[j], low)
        n = known[j]
        if j > 0:
            n = n + block_of(g, j - 1)
        xn = c2 - 2.0 * c1 + n
        yn = n - c1
        for m in range(8):
            h[m] = coef[m : m + 1] * h[m] + coef[16 + m : 17 + m] * (xn + coef[8 + m : 9 + m] * yn)
            out[j, 16 * m : 16 * m + 16] = h[m]
        out[j, 128:144] = block_of(e, j)


def final_kernel(got, fine, field, modes, total):
    for m in range(8):
        both = got[:, 16 * m : 16 * m + 16].reshape(256, 128).T
        modes[m] = both[0:64]
        modes[m + 8] = both[64:128]
    now = got[:, 128:144].reshape(256, 128).T[0:64]
    field[...] = now
    diff = now - fine[...]
    diff = diff * diff
    part = jnp.zeros((8, 128), F32)
    for x in range(8):
        part += diff[8 * x : 8 * x + 8, 0:128] + diff[8 * x : 8 * x + 8, 128:256]
    total[...] = part


def size_kernel(got, out):
    part = got[0]
    for p in range(1, 16):
        part += got[p]
    whole = jnp.sum(jnp.sum(part, axis=1, keepdims=True), axis=0, keepdims=True)
    out[...] = jnp.broadcast_to(jnp.sqrt(whole / 262144.0), (8, 128))


def ring(axis, step):
    n = lax.axis_size(axis)
    return [(i, (i + step) % n) for i in range(n)]


def swap(value, axis):
    return lax.all_to_all(value, axis, 0, 0, tiled=True)


def per_device(field, modes, source, regions, region_kappa, mode_rate, mode_weight):
    u = field.reshape(64, 256)
    h = modes.reshape(16, 64, 256)
    s = source.reshape(64, 256)
    reg = regions.reshape(64, 256)
    t = lax.axis_index("tm")
    at = jnp.stack([t, lax.axis_index("gx"), lax.axis_index("gy")]).astype(jnp.int32)

    f = jnp.exp(-0.5 * mode_rate)
    e = jnp.exp(-mode_rate)
    w = mode_weight
    omega = jnp.sum(w * (1.0 - f)).reshape(1)
    powers = jnp.exp(-mode_rate[None, :] * jnp.arange(16, dtype=F32)[:, None])
    beta = STEP * jnp.sum((w * (1.0 - e))[None, :] * powers, axis=1)
    coef = jnp.concatenate([e, f, 1.0 - f, w]).reshape(4, 2, 8).transpose(0, 2, 1)
    coef = jnp.broadcast_to(coef[..., None], (4, 8, 2, 64)).reshape(32, 128)

    plane = (64, 256)
    kap, g0, q1s, up, dn = call(local_kernel, [plane] * 3 + [(40, 256)] * 2, 7, 3)(
        region_kappa, w, w * f, u, reg, s, h
    )
    xlo = lax.ppermute(up, "gx", ring("gx", 1))
    xhi = lax.ppermute(dn, "gx", ring("gx", -1))

    sk, packed = call(scatter_pack_kernel, [(256, 128), (16, 144, 128)], 5, 1)(at, u, s, kap, h)
    far = [lax.ppermute(packed[4 * k : 4 * k + 4], "tm", [(0, 4 * k)]) for k in (1, 2, 3)]

    yup, ydn = call(side_kernel, [(80, 256)] * 2, 6, 1)(at, u, kap, g0, xlo, xhi)
    ylo = lax.ppermute(yup, "gy", ring("gy", 1))
    yhi = lax.ppermute(ydn, "gy", ring("gy", -1))

    quarter = jnp.where(t == 0, packed[0:4], far[0] + far[1] + far[2])
    close = [
        lax.ppermute(quarter[k], "tm", [(4 * a, 4 * a + k) for a in range(4)]) for k in (1, 2, 3)
    ]
    start = jnp.where(t % 4 == 0, quarter[0], close[0] + close[1] + close[2])

    fine, both = call(
        fine_kernel, [plane, (256, 128)], 10, 2, [(12, 24, 256)] * 4
    )(at, omega, u, kap, g0, q1s, xlo, xhi, ylo, yhi)
    parts = swap(both.reshape(16, 16, 128), "tm")

    msg, known = call(known_kernel, [(16, 136, 128), (16, 16, 128)], 5, 1)(
        at, parts, sk, start, coef
    )
    got = swap(msg, ("gx", "gy"))
    own, kown, up, dn = call(
        gather_kernel, [(16, 16, 8, 128), (16, 8, 128), (MSG, 8, 128), (MSG, 8, 128)], 1, 0
    )(got.reshape(16 * 136, 128))
    lo = lax.ppermute(up, "tm", ring("tm", 1))
    hi = lax.ppermute(dn, "tm", ring("tm", -1))
    out = call(
        sweep_kernel,
        [(16, 144, 128)],
        10,
        2,
        [(16 * LAY * 8, 128)] * 3 + [(7, LAY, 8, 128), (LAY, 8, 128)],
    )(at, beta, own, kown, lo, hi, parts, known, start, coef)[0]
    back = swap(out, "tm")
    new_field, new_modes, total = call(final_kernel, [plane, (16, 64, 256), (8, 128)], 2, 0)(
        back, fine
    )
    sums = swap(jnp.broadcast_to(total, (16, 8, 128)), ("gx", "gy"))
    size = call(size_kernel, [(8, 128)], 1, 0)(sums)[0]
    return (
        new_field.reshape(1, 8, 8, 256),
        new_modes.reshape(1, 16, 8, 8, 256),
        size[0, 0:1],
    )


def solution(mesh):
    return jax.shard_map(
        per_device,
        mesh=mesh,
        in_specs=(
            P("tm", "gx", "gy", None),
            P("tm", None, "gx", "gy", None),
            P("gx", "gy", None),
            P("gx", "gy", None),
            P(),
            P(),
            P(),
        ),
        out_specs=(P("tm", "gx", "gy", None), P("tm", None, "gx", "gy", None), P("tm")),
        check_vma=False,
    )
```

```python
import functools
import jax
import jax.numpy as jnp
from jax import lax
from jax.experimental import pallas as pl
from jax.experimental.pallas import tpu as pltpu
from jax.sharding import PartitionSpec as P

STEP = 0.12
F32 = jnp.float32
VM = pl.BlockSpec(memory_space=pltpu.VMEM)
SM = pl.BlockSpec(memory_space=pltpu.SMEM)
PARAMS = pltpu.CompilerParams(vmem_limit_bytes=40 * 1024 * 1024)
HALO = 15
TRI = [HALO] + [HALO - j for j in range(1, HALO)]
OFF = [sum(TRI[:j]) for j in range(HALO)]
KOFF = sum(TRI)
MSG = KOFF + HALO
LAY = 48
NEW = 46
SIZES = [0, 11, 7, 10, 10, 12, 9, 8, 10, 7, 9, 12, 11, 10, 9, 8]
BLOCKS = [(size, -(-(NEW - 2 * j) // size) if size else 0) for j, size in enumerate(SIZES)]


def call(kernel, outs, ins, smem, scratch=()):
    return pl.pallas_call(
        kernel,
        out_shape=[jax.ShapeDtypeStruct(shape, F32) for shape in outs],
        in_specs=[SM] * smem + [VM] * (ins - smem),
        out_specs=[VM] * len(outs),
        scratch_shapes=[pltpu.VMEM(shape, F32) for shape in scratch],
        compiler_params=PARAMS,
    )


def lane_low(shape):
    return lax.broadcasted_iota(jnp.int32, shape, len(shape) - 1) < 64


def local_kernel(at, rk_in, w_in, rate_in, u_in, reg_in, s_in, modes_in, u, kap, g0, q1s, up, dn, sk, packed,
                 rk, w, rate, reg, s, modes, sems):
    pairs = (
        (rk_in, rk), (w_in, w), (rate_in, rate), (modes_in, modes),
        (s_in, s), (reg_in, reg), (u_in, u),
    )
    copies = [pltpu.make_async_copy(a, b, sems.at[i]) for i, (a, b) in enumerate(pairs)]
    for copy in copies:
        copy.start()
    for copy in copies:
        copy.wait()
    half = [jnp.exp(jnp.full((8, 256), -0.5 * rate[m], F32)) for m in range(16)]
    for x in range(8):
        rows = slice(8 * x, 8 * x + 8)
        region = reg[rows]
        k = jnp.zeros((8, 256), F32)
        for r in range(8):
            k = jnp.where(region == r, rk[r], k)
        kap[rows] = k
        a = jnp.zeros((8, 256), F32)
        b = jnp.zeros((8, 256), F32)
        for m in range(16):
            h = w[m] * modes[m, rows]
            a += h
            b += half[m] * h
        g0[rows] = s[rows] - a
        q1s[rows] = s[rows] - b
    up[0:16] = u[48:64]
    up[16:32] = kap[48:64]
    up[32:40] = g0[56:64]
    dn[0:16] = u[0:16]
    dn[16:32] = kap[0:16]
    dn[32:40] = g0[0:8]
    sk[...] = jnp.concatenate([s[...], kap[...]], axis=0).T

    @pl.when(at[0] == 0)
    def _():
        for m in range(8):
            both = jnp.concatenate([modes[m], modes[m + 8]], axis=0).T
            packed[:, 16 * m : 16 * m + 16] = both.reshape(16, 16, 128)


def side_kernel(at, u, kap, g0, xlo, xhi, yup, ydn):
    has_lo = jnp.where(at[1] > 0, 1.0, 0.0).astype(F32)
    has_hi = jnp.where(at[1] < 3, 1.0, 0.0).astype(F32)
    for out, first in ((yup, 6), (ydn, 0)):
        for piece in range(5):
            if piece < 4:
                src, base = (u, 0) if piece < 2 else (kap, 16)
                y = first + piece % 2
                out[16 * piece : 16 * piece + 1] = has_lo * xlo[base + 8 + y : base + 9 + y]
                out[16 * piece + 9 : 16 * piece + 10] = has_hi * xhi[base + y : base + y + 1]
            else:
                src = g0
                y = 7 if first else 0
            for x in range(8):
                at_row = 16 * piece + 1 + x
                out[at_row : at_row + 1] = src[8 * x + y : 8 * x + y + 1]


def fine_kernel(at, omega, u, kap, g0, q1s, xlo, xhi, ylo, yhi, both, up, kp, gp, u1):
    gx, gy = at[1], at[2]
    zero = jnp.zeros((24, 256), F32)
    for ref in (up, kp, gp):
        for x in range(12):
            ref[x] = zero
    for x in range(8):
        rows = slice(8 * x, 8 * x + 8)
        up[2 + x, 8:16] = u[rows]
        kp[2 + x, 8:16] = kap[rows]
        gp[2 + x, 8:16] = g0[rows]

    @pl.when(gx > 0)
    def _():
        for i in range(2):
            up[i, 8:16] = xlo[8 * i : 8 * i + 8]
            kp[i, 8:16] = xlo[16 + 8 * i : 24 + 8 * i]
        gp[1, 8:16] = xlo[32:40]

    @pl.when(gx < 3)
    def _():
        for i in range(2):
            up[10 + i, 8:16] = xhi[8 * i : 8 * i + 8]
            kp[10 + i, 8:16] = xhi[16 + 8 * i : 24 + 8 * i]
        gp[10, 8:16] = xhi[32:40]

    for cond, ref, row in ((gy > 0, ylo, 6), (gy < 3, yhi, 16)):

        @pl.when(cond)
        def _(ref=ref, row=row):
            for x in range(10):
                for i in range(2):
                    up[1 + x, row + i : row + i + 1] = ref[16 * i + x : 16 * i + x + 1]
                    kp[1 + x, row + i : row + i + 1] = ref[32 + 16 * i + x : 33 + 16 * i + x]
                if 1 <= x <= 8:
                    near = 7 if row == 6 else 16
                    gp[1 + x, near : near + 1] = ref[64 + x : 65 + x]

    z = lax.broadcasted_iota(jnp.int32, (24, 256), 1)

    def above(v):
        return jnp.where(z == 255, 0.0, pltpu.roll(v, 255, 1))

    def below(v):
        return jnp.where(z == 0, 0.0, pltpu.roll(v, 1, 1))

    def laplace(ref, x):
        uc, kc = ref[x], kp[x]
        total = jnp.zeros((24, 256), F32)
        for near_u, near_k in (
            (ref[x + 1], kp[x + 1]),
            (ref[x - 1], kp[x - 1]),
            (pltpu.roll(uc, 23, 0), pltpu.roll(kc, 23, 0)),
            (pltpu.roll(uc, 1, 0), pltpu.roll(kc, 1, 0)),
            (above(uc), above(kc)),
            (below(uc), below(kc)),
        ):
            total += (kc + near_k) * (near_u - uc)
        return 0.5 * total

    for x in range(1, 11):
        change = (0.5 * STEP) * (laplace(up, x) + gp[x])
        u1[x] = up[x] + change
        gp[x] = change

    @pl.when(gx == 0)
    def _():
        u1[1] = zero

    @pl.when(gx == 3)
    def _():
        u1[10] = zero

    @pl.when(gy == 0)
    def _():
        for x in range(1, 11):
            u1[x, 0:8] = zero[0:8]

    @pl.when(gy == 3)
    def _():
        for x in range(1, 11):
            u1[x, 16:24] = zero[0:8]

    first, second = [], []
    for x in range(8):
        rows = slice(8 * x, 8 * x + 8)
        c1 = gp[2 + x, 8:16]
        lap = laplace(u1, 2 + x)[8:16]
        c2 = (0.5 * STEP) * (lap + q1s[rows] - omega[0] * c1)
        first.append(c1)
        second.append(c2)
    both[:, 0:16] = jnp.concatenate(first + second, axis=0).T.reshape(16, 16, 128)
    now = jnp.concatenate([u[...], u[...]], axis=0).T.reshape(16, 16, 128)
    both[:, 16:24] = jnp.where(lane_low((16, 8, 128)), now[:, 0:8], now[:, 8:16])


def doubled(v, low):
    turned = pltpu.roll(v, 64, 1)
    return jnp.where(low, v, turned), jnp.where(low, turned, v)


def unpacked(v):
    low = lane_low((8, 128))
    first, second = doubled(v, low)
    return jnp.concatenate([first, second], axis=0)


def packed_rows(v):
    return jnp.where(lane_low((8, 128)), v[0:8], v[8:16])


def known_kernel(at, parts, sk, start, coef, msg, fmsg, known):
    low = lane_low((16, 128))
    slab = sk[pl.ds(pl.multiple_of(at[0] * 16, 16), 16), :]
    source, kap = doubled(slab, low)
    h = [start[16 * m : 16 * m + 16] for m in range(8)]
    seen, fine = [], []
    for j in range(16):
        c1, c2 = doubled(parts[j, 0:16], low)
        fine.append(unpacked(parts[j, 16:24]) + c1 + c2)
        if j == 0:
            n = 2.0 * c1
            seen.append(fine[0])
        else:
            q = coef[24:25] * h[0]
            for m in range(1, 8):
                q += coef[24 + m : 25 + m] * h[m]
            n = STEP * (source - (q + pltpu.roll(q, 64, 1)))
            seen.append(n + c2 - c1)
        known[j] = n
        xn = c2 - 2.0 * c1 + n
        yn = n - c1
        for m in range(8):
            h[m] = coef[m : m + 1] * h[m] + coef[16 + m : 17 + m] * (xn + coef[8 + m : 9 + m] * yn)
    last = packed_rows(kap)
    for j in range(8):
        rows = slice(16 * j, 16 * j + 16)
        v = jnp.where(low, seen[j], seen[j + 8])
        w = jnp.where(low, fine[j], fine[j + 8])
        for p in range(16):
            msg[p, rows] = v
            fmsg[p, rows] = w
    for p in range(16):
        msg[p, 128:136] = last


def gather_kernel(got, own, kap, up, dn):
    low = lane_low((8, 128))

    def pair(row):
        even = got[pl.ds(row, 8, stride=272), :]
        odd = got[pl.ds(row + 136, 8, stride=272), :]
        left = jnp.where(low, even, pltpu.roll(odd, 64, 1))
        right = jnp.where(low, pltpu.roll(even, 64, 1), odd)
        return left, right

    def place(j, z, v):
        own[j, z] = v
        if j < HALO:
            if z < TRI[j]:
                dn[OFF[j] + z] = v
            if z >= 16 - TRI[j]:
                up[OFF[j] + z - (16 - TRI[j])] = v

    for j in range(8):
        for z in range(16):
            left, right = pair(16 * j + z)
            place(j, z, left)
            place(j + 8, z, right)
    for z in range(8):
        left, right = pair(128 + z)
        for at, v in ((z, left), (z + 8, right)):
            kap[at] = v
            if at < HALO:
                dn[KOFF + at] = v
            if at >= 1:
                up[KOFF + at - 1] = v


def sweep_kernel(at, beta, own, kown, lo, hi, e_out, g_out, v, e, g, c, kw):
    t = at[0]
    has_lo = jnp.where(t > 0, 1.0, 0.0).astype(F32)
    has_hi = jnp.where(t < 15, 1.0, 0.0).astype(F32)

    def row(j, layer):
        return pl.ds(pl.multiple_of((j * LAY + layer) * 8, 8), 8)

    zero = jnp.zeros((8, 128), F32)
    for j in range(16):
        dst = e if j == 0 else v
        if j < HALO:
            n = TRI[j]
            for i in range(n):
                dst[row(j, HALO - n + i), :] = has_lo * lo[OFF[j] + i]
                dst[row(j, 31 + i), :] = has_hi * hi[OFF[j] + i]
        for i in range(16):
            dst[row(j, 15 + i), :] = own[j, i]
    kw[0] = zero
    kw[47] = zero
    for i in range(HALO):
        kw[1 + i] = has_lo * lo[KOFF + i]
        kw[32 + i] = has_hi * hi[KOFF + i]
    for i in range(16):
        kw[16 + i] = kown[i]

    lane = lax.broadcasted_iota(jnp.int32, (8, 128), 1)
    sub = lax.broadcasted_iota(jnp.int32, (8, 128), 0)
    y, x, half = lane % 8, (lane // 8) % 8, lane // 64
    half_y, gx = sub % 2, sub // 2
    y_end, y_start = y == 7, y == 0
    x_end, x_start = x == 7, x == 0
    turn_up, turn_dn = half == 1, half == 0
    inside = (
        jnp.logical_not(x_end & (gx == 3)),
        jnp.logical_not(x_start & (gx == 0)),
        jnp.logical_not(y_end & (half == 1) & (half_y == 1)),
        jnp.logical_not(y_start & (half == 0) & (half_y == 0)),
    )

    def near(a):
        far = pltpu.roll(a, 56, 1)
        xp = jnp.where(x_end, pltpu.roll(far, 6, 0), pltpu.roll(a, 120, 1))
        far = pltpu.roll(a, 72, 1)
        xm = jnp.where(x_start, pltpu.roll(far, 2, 0), pltpu.roll(a, 8, 1))
        far = pltpu.roll(a, 71, 1)
        far = jnp.where(turn_up, pltpu.roll(far, 7, 0), far)
        yp = jnp.where(y_end, far, pltpu.roll(a, 127, 1))
        far = pltpu.roll(a, 57, 1)
        far = jnp.where(turn_dn, pltpu.roll(far, 1, 0), far)
        ym = jnp.where(y_start, far, pltpu.roll(a, 1, 1))
        return xp, xm, yp, ym

    def faces(layer):
        kc = kw[layer + 1]
        place = t * 16 - HALO + layer
        scale = jnp.where((place >= 0) & (place < 256), 0.5 * STEP, 0.0).astype(F32)
        total = zero
        for i, kn in enumerate(near(kc)):
            face = scale * (kc + jnp.where(inside[i], kn, 0.0))
            total += face
            c[i, layer] = jnp.where(inside[i], face, 0.0)
        for i, kn in ((4, kw[layer + 2]), (5, kw[layer])):
            face = scale * (kc + kn)
            total += face
            c[i, layer] = face
        c[6, layer] = -total

    for layer in range(NEW):
        faces(layer)

    for j in range(1, 16):
        block, blocks = BLOCKS[j]

        def layers(i, carry, j=j, block=block):
            for k in range(block):
                layer = j + i * block + k
                mid = e[row(j - 1, layer), :]
                acc = c[6, layer] * mid
                acc += c[4, layer] * e[row(j - 1, layer + 1), :]
                acc += c[5, layer] * e[row(j - 1, layer - 1), :]
                for d, un in enumerate(near(mid)):
                    acc += c[d, layer] * un
                for i2 in range(1, j):
                    acc -= beta[j - 1 - i2] * g[row(i2 - 1, layer), :]
                g[row(j - 1, layer), :] = acc
                e[row(j, layer), :] = mid + acc + v[row(j, layer), :]
            return carry

        lax.fori_loop(0, blocks, layers, 0)

    for j in range(16):
        for i in range(16):
            e_out[j, i] = e[row(j, HALO + i), :]
            if j > 0:
                g_out[j, i] = g[row(j - 1, HALO + i), :]
            else:
                g_out[j, i] = zero


def pack_kernel(at, got, e, g, parts, known, start, coef, out):
    p = at[1] * 4 + at[2]
    low = lane_low((16, 128))
    sublane = p // 2
    mine = low == (p % 2 == 0)

    def block_of(ref, j):
        first = j * 128 + sublane
        a = ref[pl.ds(first, 8, stride=8), :]
        b = ref[pl.ds(first + 64, 8, stride=8), :]
        both = jnp.concatenate([a, b], axis=0)
        return jnp.where(mine, both, pltpu.roll(both, 64, 1))

    h = [start[16 * m : 16 * m + 16] for m in range(8)]
    for j in range(16):
        c1, c2 = doubled(parts[j, 0:16], low)
        n = known[j] + block_of(g, j)
        xn = c2 - 2.0 * c1 + n
        yn = n - c1
        for m in range(8):
            h[m] = coef[m : m + 1] * h[m] + coef[16 + m : 17 + m] * (xn + coef[8 + m : 9 + m] * yn)
            if j % 2 == 0:
                at_row = 16 * (m % 4)
                out[j + m // 4, at_row : at_row + 16] = h[m]
        if j % 2 == 1:
            out[j - 1, 64:72] = packed_rows(xn)
            out[j, 64:72] = packed_rows(yn)
        out[j, 72:80] = packed_rows(block_of(e, j))

    half = lane_low((8, 128))
    for j in range(8):
        one = jnp.zeros((8, 128), F32)
        two = jnp.zeros((8, 128), F32)
        for z in range(16):
            even = got[pl.ds(16 * j + z, 8, stride=256), :]
            odd = got[pl.ds(16 * j + z + 128, 8, stride=256), :]
            left = jnp.where(half, even, pltpu.roll(odd, 64, 1))
            right = jnp.where(half, pltpu.roll(even, 64, 1), odd)
            at_row = (j * 16 + z) * 8
            diff = e[at_row : at_row + 8] - left
            one += diff * diff
            at_row = ((j + 8) * 16 + z) * 8
            diff = e[at_row : at_row + 8] - right
            two += diff * diff
        out[j, 80:88] = one
        out[j + 8, 80:88] = two


def final_kernel(at, got, other, coef, modes, field, size):
    def finish(low, high, odd):
        x = y = None
        if odd:
            x = jnp.concatenate([unpacked(low[t, 64:72]) for t in range(16)], axis=0)
            y = jnp.concatenate([unpacked(high[t, 64:72]) for t in range(16)], axis=0)
        for m in range(8):
            src = low if m < 4 else high
            first = 16 * (m % 4)
            both = src[:, first : first + 16].reshape(256, 128)
            if odd:
                both = coef[m : m + 1] * both
                both += coef[16 + m : 17 + m] * (x + coef[8 + m : 9 + m] * y)
            both = both.T
            modes[m] = both[0:64]
            modes[m + 8] = both[64:128]

    @pl.when(at[0] % 2 == 0)
    def _():
        finish(got, other, False)

    @pl.when(at[0] % 2 == 1)
    def _():
        finish(other, got, True)

    now = jnp.concatenate([unpacked(got[t, 72:80]) for t in range(16)], axis=0)
    field[...] = now.T[0:64]
    part = got[0, 80:88]
    for t in range(1, 16):
        part += got[t, 80:88]
    whole = jnp.sum(jnp.sum(part, axis=1, keepdims=True), axis=0, keepdims=True)
    size[...] = jnp.broadcast_to(jnp.sqrt(whole / 262144.0), (8, 128))


def ring(axis, step):
    n = lax.axis_size(axis)
    return [(i, (i + step) % n) for i in range(n)]


def swap(value, axis):
    return lax.all_to_all(value, axis, 0, 0, tiled=True)


def per_device(field, modes, source, regions, region_kappa, mode_rate, mode_weight):
    u = field.reshape(64, 256)
    h = modes.reshape(16, 64, 256)
    s = source.reshape(64, 256)
    reg = regions.reshape(64, 256)
    t = lax.axis_index("tm")
    at = jnp.stack([t, lax.axis_index("gx"), lax.axis_index("gy")]).astype(jnp.int32)

    f = jnp.exp(-0.5 * mode_rate)
    e = jnp.exp(-mode_rate)
    w = mode_weight
    omega = jnp.sum(w * (1.0 - f)).reshape(1)
    powers = jnp.exp(-mode_rate[None, :] * jnp.arange(16, dtype=F32)[:, None])
    beta = STEP * jnp.sum((w * (1.0 - e))[None, :] * powers, axis=1)
    coef = jnp.concatenate([e, f, 1.0 - f, w]).reshape(4, 2, 8).transpose(0, 2, 1)
    coef = jnp.broadcast_to(coef[..., None], (4, 8, 2, 64)).reshape(32, 128)

    plane = (64, 256)
    outs = [plane] * 4 + [(40, 256)] * 2 + [(256, 128), (16, 128, 128)]
    u, kap, g0, q1s, up, dn, sk, packed = pl.pallas_call(
        local_kernel,
        out_shape=[jax.ShapeDtypeStruct(shape, F32) for shape in outs],
        in_specs=[SM] + [pl.BlockSpec(memory_space=pl.ANY)] * 7,
        out_specs=[VM] * 8,
        scratch_shapes=[pltpu.SMEM((8,), F32), pltpu.SMEM((16,), F32), pltpu.SMEM((16,), F32)]
        + [pltpu.VMEM(plane, jnp.int32), pltpu.VMEM(plane, F32), pltpu.VMEM((16, 64, 256), F32)]
        + [pltpu.SemaphoreType.DMA((7,))],
        compiler_params=pltpu.CompilerParams(vmem_limit_bytes=60 * 1024 * 1024),
    )(at, region_kappa, w, mode_rate, u, reg, s, h)
    xlo = lax.ppermute(up, "gx", ring("gx", 1))
    xhi = lax.ppermute(dn, "gx", ring("gx", -1))
    far = [lax.ppermute(packed[4 * k : 4 * k + 4], "tm", [(0, 4 * k)]) for k in (1, 2, 3)]

    yup, ydn = call(side_kernel, [(80, 256)] * 2, 6, 1)(at, u, kap, g0, xlo, xhi)
    ylo = lax.ppermute(yup, "gy", ring("gy", 1))
    yhi = lax.ppermute(ydn, "gy", ring("gy", -1))

    quarter = jnp.where(t == 0, packed[0:4], far[0] + far[1] + far[2])
    close = [
        lax.ppermute(quarter[k], "tm", [(4 * a, 4 * a + k) for a in range(4)]) for k in (1, 2, 3)
    ]
    start = jnp.where(t % 4 == 0, quarter[0], close[0] + close[1] + close[2])

    both = call(
        fine_kernel, [(16, 24, 128)], 10, 2, [(12, 24, 256)] * 4
    )(at, omega, u, kap, g0, q1s, xlo, xhi, ylo, yhi)[0]
    parts = swap(both, "tm")

    msg, fmsg, known = call(
        known_kernel, [(16, 136, 128), (16, 128, 128), (16, 16, 128)], 5, 1
    )(at, parts, sk, start, coef)
    got = swap(msg, ("gx", "gy"))
    got, fmsg = lax.optimization_barrier((got, fmsg))
    own, kown, up, dn = call(
        gather_kernel, [(16, 16, 8, 128), (16, 8, 128), (MSG, 8, 128), (MSG, 8, 128)], 1, 0
    )(got.reshape(16 * 136, 128))
    lo = lax.ppermute(up, "tm", ring("tm", 1))
    hi = lax.ppermute(dn, "tm", ring("tm", -1))
    fine = swap(fmsg, ("gx", "gy"))
    now, grown = call(
        sweep_kernel,
        [(16, 16, 8, 128)] * 2,
        6,
        2,
        [(16 * LAY * 8, 128)] * 3 + [(7, LAY, 8, 128), (LAY, 8, 128)],
    )(at, beta, own, kown, lo, hi)
    flat = (2048, 128)
    out = call(pack_kernel, [(16, 88, 128)], 8, 1)(
        at, fine.reshape(flat), now.reshape(flat), grown.reshape(flat), parts, known, start, coef
    )[0]
    back = swap(out, "tm")
    other = lax.ppermute(back, "tm", [(i, i ^ 1) for i in range(16)])
    new_modes, new_field, size = call(
        final_kernel, [(16, 64, 256), plane, (8, 128)], 4, 1
    )(at, back, other, coef)
    return (
        new_field.reshape(1, 8, 8, 256),
        new_modes.reshape(1, 16, 8, 8, 256),
        size[0, 0:1],
    )


def solution(mesh):
    return jax.shard_map(
        per_device,
        mesh=mesh,
        in_specs=(
            P("tm", "gx", "gy", None),
            P("tm", None, "gx", "gy", None),
            P("gx", "gy", None),
            P("gx", "gy", None),
            P(),
            P(),
            P(),
        ),
        out_specs=(P("tm", "gx", "gy", None), P("tm", None, "gx", "gy", None), P("tm")),
        check_vma=False,
    )
```

```python
import functools
import jax
import jax.numpy as jnp
from jax import lax
from jax.experimental import pallas as pl
from jax.experimental.pallas import tpu as pltpu
from jax.sharding import PartitionSpec as P

STEP = 0.12
F32 = jnp.float32
VM = pl.BlockSpec(memory_space=pltpu.VMEM)
SM = pl.BlockSpec(memory_space=pltpu.SMEM)
ANY = pl.BlockSpec(memory_space=pl.ANY)
MIB = 1024 * 1024
HALO = 15
TRI = [HALO] + [HALO - j for j in range(1, HALO)]
OFF = [sum(TRI[:j]) for j in range(HALO)]
KOFF = sum(TRI)
MSG = KOFF + HALO
LAY = 48
NEW = 46
GROUP = 16


def call(kernel, outs, ins, smem, scratch=(), limit=16):
    return pl.pallas_call(
        kernel,
        out_shape=[jax.ShapeDtypeStruct(shape, F32) for shape in outs],
        in_specs=[SM] * smem + [VM] * (ins - smem),
        out_specs=[VM] * len(outs),
        scratch_shapes=[pltpu.VMEM(shape, F32) for shape in scratch],
        compiler_params=pltpu.CompilerParams(vmem_limit_bytes=limit * MIB),
    )


def lane_low(shape):
    return lax.broadcasted_iota(jnp.int32, shape, len(shape) - 1) < 64


def local_kernel(rk_in, w_in, rate_in, u_in, reg_in, s_in, modes_in, u, kap, g0, q1s, up, dn, sk,
                 rk, w, rate, reg, s, modes, sems):
    pairs = [(u_in, u), (reg_in, reg), (s_in, s), (rk_in, rk), (w_in, w), (rate_in, rate)]
    pairs += [(modes_in.at[pl.ds(4 * i, 4)], modes.at[pl.ds(4 * i, 4)]) for i in range(4)]
    copies = [pltpu.make_async_copy(a, b, sems.at[i]) for i, (a, b) in enumerate(pairs)]
    for copy in copies:
        copy.start()
    for copy in copies[:6]:
        copy.wait()
    for x in range(8):
        rows = slice(8 * x, 8 * x + 8)
        region = reg[rows]
        k = jnp.zeros((8, 256), F32)
        for r in range(8):
            k = jnp.where(region == r, rk[r], k)
        kap[rows] = k
    half = [jnp.exp(jnp.full((8, 256), -0.5 * rate[m], F32)) for m in range(16)]
    a = [s[8 * x : 8 * x + 8] for x in range(8)]
    b = [s[8 * x : 8 * x + 8] for x in range(8)]
    for m in range(16):
        if m % 4 == 0:
            copies[6 + m // 4].wait()
        for x in range(8):
            h = w[m] * modes[m, 8 * x : 8 * x + 8]
            a[x] = a[x] - h
            b[x] = b[x] - half[m] * h
    for x in range(8):
        g0[8 * x : 8 * x + 8] = a[x]
        q1s[8 * x : 8 * x + 8] = b[x]
    up[0:16] = u[48:64]
    up[16:32] = kap[48:64]
    up[32:40] = g0[56:64]
    dn[0:16] = u[0:16]
    dn[16:32] = kap[0:16]
    dn[32:40] = g0[0:8]
    sk[...] = jnp.concatenate([s[...], kap[...]], axis=0).T


def scatter_kernel(after, modes_in, out0, out1, out2, out3, modes, packed, sems):
    @pl.when(lax.axis_index("tm") == 0)
    def _():
        copies = [
            pltpu.make_async_copy(modes_in.at[pl.ds(4 * i, 4)], modes.at[pl.ds(4 * i, 4)], sems.at[i])
            for i in range(4)
        ]
        for copy in copies:
            copy.start()
        for copy in copies:
            copy.wait()
        for m in range(8):
            both = jnp.concatenate([modes[m], modes[m + 8]], axis=0).T
            packed[:, 16 * m : 16 * m + 16] = both.reshape(16, 16, 128)
        copies = [
            pltpu.make_async_copy(packed.at[pl.ds(4 * i, 4)], out, sems.at[4 + i])
            for i, out in enumerate((out0, out1, out2, out3))
        ]
        for copy in copies:
            copy.start()
        for copy in copies:
            copy.wait()


def side_kernel(u, kap, g0, xlo, xhi, yup, ydn):
    has_lo = jnp.where(lax.axis_index("gx") > 0, 1.0, 0.0).astype(F32)
    has_hi = jnp.where(lax.axis_index("gx") < 3, 1.0, 0.0).astype(F32)
    for out, first in ((yup, 6), (ydn, 0)):
        for piece in range(5):
            if piece < 4:
                src, base = (u, 0) if piece < 2 else (kap, 16)
                y = first + piece % 2
                out[16 * piece : 16 * piece + 1] = has_lo * xlo[base + 8 + y : base + 9 + y]
                out[16 * piece + 9 : 16 * piece + 10] = has_hi * xhi[base + y : base + y + 1]
            else:
                src = g0
                y = 7 if first else 0
            for x in range(8):
                at_row = 16 * piece + 1 + x
                out[at_row : at_row + 1] = src[8 * x + y : 8 * x + y + 1]


def fine_kernel(omega, u, kap, g0, q1s, xlo, xhi, ylo, yhi, fine, both, up, kp, gp, u1):
    gx, gy = lax.axis_index("gx"), lax.axis_index("gy")
    zero = jnp.zeros((24, 256), F32)
    for ref in (up, kp, gp):
        for x in range(12):
            ref[x] = zero
    for x in range(8):
        rows = slice(8 * x, 8 * x + 8)
        up[2 + x, 8:16] = u[rows]
        kp[2 + x, 8:16] = kap[rows]
        gp[2 + x, 8:16] = g0[rows]

    @pl.when(gx > 0)
    def _():
        for i in range(2):
            up[i, 8:16] = xlo[8 * i : 8 * i + 8]
            kp[i, 8:16] = xlo[16 + 8 * i : 24 + 8 * i]
        gp[1, 8:16] = xlo[32:40]

    @pl.when(gx < 3)
    def _():
        for i in range(2):
            up[10 + i, 8:16] = xhi[8 * i : 8 * i + 8]
            kp[10 + i, 8:16] = xhi[16 + 8 * i : 24 + 8 * i]
        gp[10, 8:16] = xhi[32:40]

    for cond, ref, row in ((gy > 0, ylo, 6), (gy < 3, yhi, 16)):

        @pl.when(cond)
        def _(ref=ref, row=row):
            for x in range(10):
                for i in range(2):
                    up[1 + x, row + i : row + i + 1] = ref[16 * i + x : 16 * i + x + 1]
                    kp[1 + x, row + i : row + i + 1] = ref[32 + 16 * i + x : 33 + 16 * i + x]
                if 1 <= x <= 8:
                    near = 7 if row == 6 else 16
                    gp[1 + x, near : near + 1] = ref[64 + x : 65 + x]

    z = lax.broadcasted_iota(jnp.int32, (24, 256), 1)

    def above(v):
        return jnp.where(z == 255, 0.0, pltpu.roll(v, 255, 1))

    def below(v):
        return jnp.where(z == 0, 0.0, pltpu.roll(v, 1, 1))

    def laplace(ref, x):
        uc, kc = ref[x], kp[x]
        total = jnp.zeros((24, 256), F32)
        for near_u, near_k in (
            (ref[x + 1], kp[x + 1]),
            (ref[x - 1], kp[x - 1]),
            (pltpu.roll(uc, 23, 0), pltpu.roll(kc, 23, 0)),
            (pltpu.roll(uc, 1, 0), pltpu.roll(kc, 1, 0)),
            (above(uc), above(kc)),
            (below(uc), below(kc)),
        ):
            total += (kc + near_k) * (near_u - uc)
        return 0.5 * total

    for x in range(1, 11):
        change = (0.5 * STEP) * (laplace(up, x) + gp[x])
        u1[x] = up[x] + change
        gp[x] = change

    @pl.when(gx == 0)
    def _():
        u1[1] = zero

    @pl.when(gx == 3)
    def _():
        u1[10] = zero

    @pl.when(gy == 0)
    def _():
        for x in range(1, 11):
            u1[x, 0:8] = zero[0:8]

    @pl.when(gy == 3)
    def _():
        for x in range(1, 11):
            u1[x, 16:24] = zero[0:8]

    first, second = [], []
    for x in range(8):
        rows = slice(8 * x, 8 * x + 8)
        c1 = gp[2 + x, 8:16]
        lap = laplace(u1, 2 + x)[8:16]
        c2 = (0.5 * STEP) * (lap + q1s[rows] - omega[0] * c1)
        fine[rows] = u1[2 + x, 8:16] + c2
        first.append(c1)
        second.append(c2)
    both[:, 0:16] = jnp.concatenate(first + second, axis=0).T.reshape(16, 16, 128)
    now = jnp.concatenate([u[...], u[...]], axis=0).T.reshape(16, 16, 128)
    both[:, 16:24] = jnp.where(lane_low((16, 8, 128)), now[:, 0:8], now[:, 8:16])


def doubled(v, low):
    turned = pltpu.roll(v, 64, 1)
    return jnp.where(low, v, turned), jnp.where(low, turned, v)


def unpacked(v):
    low = lane_low((8, 128))
    first, second = doubled(v, low)
    return jnp.concatenate([first, second], axis=0)


def packed_rows(v):
    return jnp.where(lane_low((8, 128)), v[0:8], v[8:16])


def known_kernel(parts, sk, start, coef, msg, known):
    low = lane_low((16, 128))
    slab = sk[pl.ds(pl.multiple_of(lax.axis_index("tm") * 16, 16), 16), :]
    source, kap = doubled(slab, low)
    h = [start[16 * m : 16 * m + 16] for m in range(8)]
    seen = []
    for j in range(16):
        c1, c2 = doubled(parts[j, 0:16], low)
        if j == 0:
            n = 2.0 * c1
            seen.append(unpacked(parts[0, 16:24]) + c1 + c2)
        else:
            q = coef[24:25] * h[0]
            for m in range(1, 8):
                q += coef[24 + m : 25 + m] * h[m]
            n = STEP * (source - (q + pltpu.roll(q, 64, 1)))
            seen.append(n + c2 - c1)
        known[j] = n
        xn = c2 - 2.0 * c1 + n
        yn = n - c1
        for m in range(8):
            h[m] = coef[m : m + 1] * h[m] + coef[16 + m : 17 + m] * (xn + coef[8 + m : 9 + m] * yn)
    last = packed_rows(kap)
    for j in range(8):
        v = jnp.where(low, seen[j], seen[j + 8])
        for p in range(16):
            msg[p, 16 * j : 16 * j + 16] = v
    for p in range(16):
        msg[p, 128:136] = last


def gather_kernel(got, own, kap, up, dn):
    low = lane_low((8, 128))

    def pair(row):
        even = got[pl.ds(row, 8, stride=272), :]
        odd = got[pl.ds(row + 136, 8, stride=272), :]
        left = jnp.where(low, even, pltpu.roll(odd, 64, 1))
        right = jnp.where(low, pltpu.roll(even, 64, 1), odd)
        return left, right

    def place(j, z, v):
        own[j, z] = v
        if j < HALO:
            if z < TRI[j]:
                dn[OFF[j] + z] = v
            if z >= 16 - TRI[j]:
                up[OFF[j] + z - (16 - TRI[j])] = v

    for j in range(8):
        for z in range(16):
            left, right = pair(16 * j + z)
            place(j, z, left)
            place(j + 8, z, right)
    for z in range(8):
        left, right = pair(128 + z)
        for at, v in ((z, left), (z + 8, right)):
            kap[at] = v
            if at < HALO:
                dn[KOFF + at] = v
            if at >= 1:
                up[KOFF + at - 1] = v


def sweep_kernel(beta, own, kown, lo, hi, parts_in, known_in, start_in, coef_in, out,
                 e, g, c, kw, parts, known, start, coef, sems):
    pairs = ((parts_in, parts), (known_in, known), (start_in, start), (coef_in, coef))
    copies = [pltpu.make_async_copy(a, b, sems.at[i]) for i, (a, b) in enumerate(pairs)]
    for copy in copies:
        copy.start()
    t = lax.axis_index("tm")
    has_lo = jnp.where(t > 0, 1.0, 0.0).astype(F32)
    has_hi = jnp.where(t < 15, 1.0, 0.0).astype(F32)

    def pick(j, first, last):
        if last <= HALO:
            start = OFF[j] + first - HALO + TRI[j]
            return has_lo * lo[start : start + last - first]
        if first > 30:
            start = OFF[j] + first - 31
            return has_hi * hi[start : start + last - first]
        return own[j, first - HALO : last - HALO]

    def groups(first, last):
        ranges = []
        for a, b in ((first, HALO), (HALO, 31), (31, last)):
            pieces = -(-(b - a) // GROUP)
            edge = [a + (b - a) * k // pieces for k in range(pieces + 1)] if pieces else []
            ranges += list(zip(edge[:-1], edge[1:]))
        return ranges

    zero = jnp.zeros((8, 128), F32)
    kw[0] = zero
    kw[47] = zero
    kw[1:16] = has_lo * lo[KOFF:MSG]
    kw[16:32] = kown[...]
    kw[32:47] = has_hi * hi[KOFF:MSG]

    lane = lax.broadcasted_iota(jnp.int32, (8, 128), 1)
    sub = lax.broadcasted_iota(jnp.int32, (8, 128), 0)
    x_start, x_end = lane < 8, lane >= 120
    y_start, y_end = lane % 8 == 0, lane % 8 == 7
    inside = (
        jnp.logical_not(x_end & (sub % 2 == 1)),
        jnp.logical_not(x_start & (sub % 2 == 0)),
        jnp.logical_not(y_end & (sub // 2 == 3)),
        jnp.logical_not(y_start & (sub // 2 == 0)),
    )

    def near(a):
        down, up = pltpu.roll(a, 8, 2), pltpu.roll(a, 120, 2)
        xm = jnp.where(x_start, pltpu.roll(down, 1, 1), down)
        xp = jnp.where(x_end, pltpu.roll(up, 7, 1), up)
        yp = pltpu.roll(jnp.where(y_start, pltpu.roll(down, 6, 1), a), 127, 2)
        ym = pltpu.roll(jnp.where(y_end, pltpu.roll(up, 2, 1), a), 1, 2)
        return xp, xm, yp, ym

    for first, last in groups(1, NEW - 1):
        kc = kw[first + 1 : last + 1]
        layer = lax.broadcasted_iota(jnp.int32, kc.shape, 0) + first
        place = t * 16 - HALO + layer
        scale = jnp.where((place >= 0) & (place < 256), 0.5 * STEP, 0.0).astype(F32)
        total = jnp.zeros_like(kc)
        for i, kn in enumerate(near(kc)):
            face = scale * (kc + jnp.where(inside[i], kn, 0.0))
            total += face
            c[i, first:last] = jnp.where(inside[i], face, 0.0)
        for i, kn in ((4, kw[first + 2 : last + 2]), (5, kw[first:last])):
            face = scale * (kc + kn)
            total += face
            c[i, first:last] = face
        c[6, first:last] = -total

    for first, last in groups(0, NEW):
        e[0, first:last] = pick(0, first, last)
    for j in range(1, 16):
        for first, last in groups(j, NEW - j):
            mid = e[j - 1, first:last]
            acc = c[6, first:last] * mid
            acc += c[4, first:last] * e[j - 1, first + 1 : last + 1]
            acc += c[5, first:last] * e[j - 1, first - 1 : last - 1]
            for d, un in enumerate(near(mid)):
                acc += c[d, first:last] * un
            for i in range(1, j):
                acc -= beta[j - 1 - i] * g[i, first:last]
            now = mid + acc + pick(j, first, last)
            g[j, first:last] = acc
            e[j, first:last] = now
    for copy in copies:
        copy.wait()
    low = lane_low((16, 128))
    p = lax.axis_index("gy") * 4 + lax.axis_index("gx")
    sublane = p // 2
    mine = low == (p % 2 == 0)
    e_rows = e.reshape(16 * LAY * 8, 128)
    g_rows = g.reshape(16 * LAY * 8, 128)

    def block_of(ref, j):
        first = (j * LAY + HALO) * 8 + sublane
        a = ref[pl.ds(first, 8, stride=8), :]
        b = ref[pl.ds(first + 64, 8, stride=8), :]
        both = jnp.concatenate([a, b], axis=0)
        return jnp.where(mine, both, pltpu.roll(both, 64, 1))

    h = [start[16 * m : 16 * m + 16] for m in range(8)]
    for j in range(16):
        c1, c2 = doubled(parts[j, 0:16], low)
        n = known[j]
        if j > 0:
            n = n + block_of(g_rows, j)
        xn = c2 - 2.0 * c1 + n
        yn = n - c1
        for m in range(8):
            h[m] = coef[m : m + 1] * h[m] + coef[16 + m : 17 + m] * (xn + coef[8 + m : 9 + m] * yn)
            if j % 2 == 0:
                at_row = 16 * (m % 4)
                out[j + m // 4, at_row : at_row + 16] = h[m]
        out[j, 64:72] = packed_rows(block_of(e_rows, j))


def rows_of(ref):
    return jnp.concatenate([unpacked(ref[t, 64:72]) for t in range(16)], axis=0)


def field_kernel(got, fine, field, part):
    now = rows_of(got).T[0:64]
    field[...] = now
    diff = now - fine[...]
    diff = diff * diff
    total = jnp.zeros((8, 128), F32)
    for x in range(8):
        total += diff[8 * x : 8 * x + 8, 0:128] + diff[8 * x : 8 * x + 8, 128:256]
    for p in range(16):
        part[p] = total


def final_kernel(got, other, mine, coef, modes):
    def finish(low, high, odd):
        x = y = None
        if odd:
            c1, c2 = doubled(mine[:, 0:16].reshape(256, 128), lane_low((256, 128)))
            x = rows_of(high) - rows_of(low) - c1
            y = x - c2 + c1
        for m in range(8):
            src = low if m < 4 else high
            first = 16 * (m % 4)
            both = src[:, first : first + 16].reshape(256, 128)
            if odd:
                both = coef[m : m + 1] * both
                both += coef[16 + m : 17 + m] * (x + coef[8 + m : 9 + m] * y)
            both = both.T
            modes[m] = both[0:64]
            modes[m + 8] = both[64:128]

    t = lax.axis_index("tm")

    @pl.when(t % 2 == 0)
    def _():
        finish(got, other, False)

    @pl.when(t % 2 == 1)
    def _():
        finish(other, got, True)


def ring(axis, step):
    n = lax.axis_size(axis)
    return [(i, (i + step) % n) for i in range(n)]


def swap(value, axis):
    return lax.all_to_all(value, axis, 0, 0, tiled=True)


def per_device(field, modes, source, regions, region_kappa, mode_rate, mode_weight):
    u = field.reshape(64, 256)
    h = modes.reshape(16, 64, 256)
    s = source.reshape(64, 256)
    reg = regions.reshape(64, 256)
    t = lax.axis_index("tm")

    f = jnp.exp(-0.5 * mode_rate)
    e = jnp.exp(-mode_rate)
    w = mode_weight
    omega = jnp.sum(w * (1.0 - f)).reshape(1)
    powers = jnp.exp(-mode_rate[None, :] * jnp.arange(16, dtype=F32)[:, None])
    beta = STEP * jnp.sum((w * (1.0 - e))[None, :] * powers, axis=1)
    coef = jnp.concatenate([e, f, 1.0 - f, w]).reshape(4, 2, 8).transpose(0, 2, 1)
    coef = jnp.broadcast_to(coef[..., None], (4, 8, 2, 64)).reshape(32, 128)

    plane = (64, 256)
    outs = [plane] * 4 + [(40, 256)] * 2 + [(256, 128)]
    u, kap, g0, q1s, up, dn, sk = pl.pallas_call(
        local_kernel,
        out_shape=[jax.ShapeDtypeStruct(shape, F32) for shape in outs],
        in_specs=[ANY] * 7,
        out_specs=[VM] * 7,
        scratch_shapes=[pltpu.SMEM((8,), F32), pltpu.SMEM((16,), F32), pltpu.SMEM((16,), F32)]
        + [pltpu.VMEM(plane, jnp.int32), pltpu.VMEM(plane, F32), pltpu.VMEM((16, 64, 256), F32)]
        + [pltpu.SemaphoreType.DMA((10,))],
        compiler_params=pltpu.CompilerParams(vmem_limit_bytes=60 * MIB),
    )(region_kappa, w, mode_rate, u, reg, s, h)
    xlo = lax.ppermute(up, "gx", ring("gx", 1))
    xhi = lax.ppermute(dn, "gx", ring("gx", -1))
    chunks = pl.pallas_call(
        scatter_kernel,
        out_shape=[jax.ShapeDtypeStruct((4, 128, 128), F32)] * 4,
        in_specs=[ANY, ANY],
        out_specs=[ANY] * 4,
        scratch_shapes=[pltpu.VMEM((16, 64, 256), F32), pltpu.VMEM((16, 128, 128), F32)]
        + [pltpu.SemaphoreType.DMA((8,))],
        compiler_params=pltpu.CompilerParams(vmem_limit_bytes=60 * MIB),
    )(sk, h)

    yup, ydn = call(side_kernel, [(80, 256)] * 2, 5, 0)(u, kap, g0, xlo, xhi)
    ylo = lax.ppermute(yup, "gy", ring("gy", 1))
    yhi = lax.ppermute(ydn, "gy", ring("gy", -1))
    far = [lax.ppermute(chunks[k], "tm", [(0, 4 * k)]) for k in (1, 2, 3)]

    fine, both = call(
        fine_kernel, [plane, (16, 24, 128)], 9, 1, [(12, 24, 256)] * 4
    )(omega, u, kap, g0, q1s, xlo, xhi, ylo, yhi)
    parts = swap(both, "tm")

    quarter = jnp.where(t == 0, chunks[0], far[0] + far[1] + far[2])
    close = [
        lax.ppermute(quarter[k], "tm", [(4 * a, 4 * a + k) for a in range(4)]) for k in (1, 2, 3)
    ]
    start = jnp.where(t % 4 == 0, quarter[0], close[0] + close[1] + close[2])

    msg, known = call(known_kernel, [(16, 136, 128), (16, 16, 128)], 4, 0)(
        parts, sk, start, coef
    )
    got = swap(msg, ("gy", "gx"))
    own, kown, up, dn = call(
        gather_kernel, [(16, 16, 8, 128), (16, 8, 128), (MSG, 8, 128), (MSG, 8, 128)], 1, 0
    )(got.reshape(16 * 136, 128))
    lo = lax.ppermute(up, "tm", ring("tm", 1))
    hi = lax.ppermute(dn, "tm", ring("tm", -1))
    out = pl.pallas_call(
        sweep_kernel,
        out_shape=jax.ShapeDtypeStruct((16, 72, 128), F32),
        in_specs=[SM] + [VM] * 4 + [ANY] * 4,
        out_specs=VM,
        scratch_shapes=[
            pltpu.VMEM(shape, F32)
            for shape in (
                (16, LAY, 8, 128),
                (16, LAY, 8, 128),
                (7, LAY, 8, 128),
                (LAY, 8, 128),
                (16, 24, 128),
                (16, 16, 128),
                (128, 128),
                (32, 128),
            )
        ]
        + [pltpu.SemaphoreType.DMA((4,))],
        compiler_params=pltpu.CompilerParams(vmem_limit_bytes=24 * MIB),
    )(beta, own, kown, lo, hi, parts, known, start, coef)
    back = swap(out, "tm")
    other = lax.ppermute(back, "tm", [(i, i ^ 1) for i in range(16)])
    new_field, part = call(field_kernel, [plane, (16, 8, 128)], 2, 0)(back, fine)
    parted = swap(part, ("gy", "gx"))
    new_modes = call(final_kernel, [(16, 64, 256)], 4, 0)(back, other, both, coef)[0]
    parted, new_modes = lax.optimization_barrier((parted, new_modes))
    size = jnp.sqrt(jnp.sum(parted) / 262144.0).reshape(1)
    return (new_field.reshape(1, 8, 8, 256), new_modes.reshape(1, 16, 8, 8, 256), size)


def solution(mesh):
    return jax.shard_map(
        per_device,
        mesh=mesh,
        in_specs=(
            P("tm", "gx", "gy", None),
            P("tm", None, "gx", "gy", None),
            P("gx", "gy", None),
            P("gx", "gy", None),
            P(),
            P(),
            P(),
        ),
        out_specs=(P("tm", "gx", "gy", None), P("tm", None, "gx", "gy", None), P("tm")),
        check_vma=False,
    )
```

```python
import functools
import jax
import jax.numpy as jnp
from jax import lax
from jax.experimental import pallas as pl
from jax.experimental.pallas import tpu as pltpu
from jax.sharding import PartitionSpec as P

STEP = 0.12
F32 = jnp.float32
VM = pl.BlockSpec(memory_space=pltpu.VMEM)
SM = pl.BlockSpec(memory_space=pltpu.SMEM)
ANY = pl.BlockSpec(memory_space=pl.ANY)
MIB = 1024 * 1024
LONG = pl.CostEstimate(flops=20_000_000_000, bytes_accessed=1_000_000, transcendentals=0)
SLOTS = [0, 1, 2, 3, 0, 0, 4, 5, 6, 7, 8, 9, 12, 13, 14, 15, 11, 10]
HALO = 15
TRI = [HALO] + [HALO - j for j in range(1, HALO)]
OFF = [sum(TRI[:j]) for j in range(HALO)]
KOFF = sum(TRI)
MSG = KOFF + HALO
LAY = 48
NEW = 46
GROUP = 16


def call(kernel, outs, ins, smem, scratch=(), limit=16, cost=None):
    return pl.pallas_call(
        kernel,
        out_shape=[jax.ShapeDtypeStruct(shape, F32) for shape in outs],
        in_specs=[SM] * smem + [VM] * (ins - smem),
        out_specs=[VM] * len(outs),
        scratch_shapes=[pltpu.VMEM(shape, F32) for shape in scratch],
        compiler_params=pltpu.CompilerParams(vmem_limit_bytes=limit * MIB),
        cost_estimate=cost,
    )


def lane_low(shape):
    return lax.broadcasted_iota(jnp.int32, shape, len(shape) - 1) < 64


def local_kernel(rk_in, w_in, rate_in, u_in, reg_in, s_in, modes_in, u, kap, g0, q1s, up, dn, sk,
                 rk, w, rate, reg, s, modes, sems):
    pairs = [(u_in, u), (reg_in, reg), (s_in, s), (rk_in, rk), (w_in, w), (rate_in, rate)]
    pairs += [(modes_in.at[pl.ds(4 * i, 4)], modes.at[pl.ds(4 * i, 4)]) for i in range(4)]
    copies = [pltpu.make_async_copy(a, b, sems.at[i]) for i, (a, b) in enumerate(pairs)]
    for copy in copies:
        copy.start()
    for copy in copies[:6]:
        copy.wait()
    for x in range(8):
        rows = slice(8 * x, 8 * x + 8)
        region = reg[rows]
        k = jnp.zeros((8, 256), F32)
        for r in range(8):
            k = jnp.where(region == r, rk[r], k)
        kap[rows] = k
    half = [jnp.exp(jnp.full((8, 256), -0.5 * rate[m], F32)) for m in range(16)]
    a = [s[8 * x : 8 * x + 8] for x in range(8)]
    b = [s[8 * x : 8 * x + 8] for x in range(8)]
    for m in range(16):
        if m % 4 == 0:
            copies[6 + m // 4].wait()
        for x in range(8):
            h = w[m] * modes[m, 8 * x : 8 * x + 8]
            a[x] = a[x] - h
            b[x] = b[x] - half[m] * h
    for x in range(8):
        g0[8 * x : 8 * x + 8] = a[x]
        q1s[8 * x : 8 * x + 8] = b[x]
    up[0:16] = u[48:64]
    up[16:32] = kap[48:64]
    up[32:40] = g0[56:64]
    dn[0:16] = u[0:16]
    dn[16:32] = kap[0:16]
    dn[32:40] = g0[0:8]
    sk[...] = jnp.concatenate([s[...], kap[...]], axis=0).T


def scatter_kernel(after, modes_in, out0, out1, out2, modes, packed, sems):
    @pl.when(lax.axis_index("tm") == 0)
    def _():
        copies = [
            pltpu.make_async_copy(modes_in.at[pl.ds(4 * i, 4)], modes.at[pl.ds(4 * i, 4)], sems.at[i])
            for i in range(4)
        ]
        for copy in copies:
            copy.start()
        for copy in copies:
            copy.wait()
        for m in range(8):
            both = jnp.concatenate([modes[m], modes[m + 8]], axis=0).T
            pieces = both.reshape(16, 16, 128)
            for place, slot in enumerate(SLOTS):
                packed[place, 16 * m : 16 * m + 16] = pieces[slot]
        copies = [
            pltpu.make_async_copy(packed.at[pl.ds(6 * i, 6)], out, sems.at[4 + i])
            for i, out in enumerate((out0, out1, out2))
        ]
        for copy in copies:
            copy.start()
        for copy in copies:
            copy.wait()


def side_kernel(u, kap, g0, xlo, xhi, yup, ydn):
    has_lo = jnp.where(lax.axis_index("gx") > 0, 1.0, 0.0).astype(F32)
    has_hi = jnp.where(lax.axis_index("gx") < 3, 1.0, 0.0).astype(F32)
    for out, first in ((yup, 6), (ydn, 0)):
        for piece in range(5):
            if piece < 4:
                src, base = (u, 0) if piece < 2 else (kap, 16)
                y = first + piece % 2
                out[16 * piece : 16 * piece + 1] = has_lo * xlo[base + 8 + y : base + 9 + y]
                out[16 * piece + 9 : 16 * piece + 10] = has_hi * xhi[base + y : base + y + 1]
            else:
                src = g0
                y = 7 if first else 0
            for x in range(8):
                at_row = 16 * piece + 1 + x
                out[at_row : at_row + 1] = src[8 * x + y : 8 * x + y + 1]


def fine_kernel(omega, u, kap, g0, q1s, xlo, xhi, ylo, yhi, fine, both, up, kp, gp, u1):
    gx, gy = lax.axis_index("gx"), lax.axis_index("gy")
    zero = jnp.zeros((24, 256), F32)
    for ref in (up, kp, gp):
        for x in range(12):
            ref[x] = zero
    for x in range(8):
        rows = slice(8 * x, 8 * x + 8)
        up[2 + x, 8:16] = u[rows]
        kp[2 + x, 8:16] = kap[rows]
        gp[2 + x, 8:16] = g0[rows]

    @pl.when(gx > 0)
    def _():
        for i in range(2):
            up[i, 8:16] = xlo[8 * i : 8 * i + 8]
            kp[i, 8:16] = xlo[16 + 8 * i : 24 + 8 * i]
        gp[1, 8:16] = xlo[32:40]

    @pl.when(gx < 3)
    def _():
        for i in range(2):
            up[10 + i, 8:16] = xhi[8 * i : 8 * i + 8]
            kp[10 + i, 8:16] = xhi[16 + 8 * i : 24 + 8 * i]
        gp[10, 8:16] = xhi[32:40]

    for cond, ref, row in ((gy > 0, ylo, 6), (gy < 3, yhi, 16)):

        @pl.when(cond)
        def _(ref=ref, row=row):
            for x in range(10):
                for i in range(2):
                    up[1 + x, row + i : row + i + 1] = ref[16 * i + x : 16 * i + x + 1]
                    kp[1 + x, row + i : row + i + 1] = ref[32 + 16 * i + x : 33 + 16 * i + x]
                if 1 <= x <= 8:
                    near = 7 if row == 6 else 16
                    gp[1 + x, near : near + 1] = ref[64 + x : 65 + x]

    z = lax.broadcasted_iota(jnp.int32, (24, 256), 1)

    def above(v):
        return jnp.where(z == 255, 0.0, pltpu.roll(v, 255, 1))

    def below(v):
        return jnp.where(z == 0, 0.0, pltpu.roll(v, 1, 1))

    def laplace(ref, x):
        uc, kc = ref[x], kp[x]
        total = jnp.zeros((24, 256), F32)
        for near_u, near_k in (
            (ref[x + 1], kp[x + 1]),
            (ref[x - 1], kp[x - 1]),
            (pltpu.roll(uc, 23, 0), pltpu.roll(kc, 23, 0)),
            (pltpu.roll(uc, 1, 0), pltpu.roll(kc, 1, 0)),
            (above(uc), above(kc)),
            (below(uc), below(kc)),
        ):
            total += (kc + near_k) * (near_u - uc)
        return 0.5 * total

    for x in range(1, 11):
        change = (0.5 * STEP) * (laplace(up, x) + gp[x])
        u1[x] = up[x] + change
        gp[x] = change

    @pl.when(gx == 0)
    def _():
        u1[1] = zero

    @pl.when(gx == 3)
    def _():
        u1[10] = zero

    @pl.when(gy == 0)
    def _():
        for x in range(1, 11):
            u1[x, 0:8] = zero[0:8]

    @pl.when(gy == 3)
    def _():
        for x in range(1, 11):
            u1[x, 16:24] = zero[0:8]

    first, second = [], []
    for x in range(8):
        rows = slice(8 * x, 8 * x + 8)
        c1 = gp[2 + x, 8:16]
        lap = laplace(u1, 2 + x)[8:16]
        c2 = (0.5 * STEP) * (lap + q1s[rows] - omega[0] * c1)
        fine[rows] = u1[2 + x, 8:16] + c2
        first.append(c1)
        second.append(c2)
    both[:, 0:16] = jnp.concatenate(first + second, axis=0).T.reshape(16, 16, 128)
    now = jnp.concatenate([u[...], u[...]], axis=0).T.reshape(16, 16, 128)
    both[:, 16:24] = jnp.where(lane_low((16, 8, 128)), now[:, 0:8], now[:, 8:16])


def doubled(v, low):
    turned = pltpu.roll(v, 64, 1)
    return jnp.where(low, v, turned), jnp.where(low, turned, v)


def unpacked(v):
    low = lane_low((8, 128))
    first, second = doubled(v, low)
    return jnp.concatenate([first, second], axis=0)


def packed_rows(v):
    return jnp.where(lane_low((8, 128)), v[0:8], v[8:16])


def known_kernel(parts, sk, start, coef, msg, known):
    low = lane_low((16, 128))
    slab = sk[pl.ds(pl.multiple_of(lax.axis_index("tm") * 16, 16), 16), :]
    source, kap = doubled(slab, low)
    h = [start[16 * m : 16 * m + 16] for m in range(8)]
    seen = []
    for j in range(16):
        c1, c2 = doubled(parts[j, 0:16], low)
        if j == 0:
            n = 2.0 * c1
            seen.append(unpacked(parts[0, 16:24]) + c1 + c2)
        else:
            q = coef[24:25] * h[0]
            for m in range(1, 8):
                q += coef[24 + m : 25 + m] * h[m]
            n = STEP * (source - (q + pltpu.roll(q, 64, 1)))
            seen.append(n + c2 - c1)
        known[j] = n
        xn = c2 - 2.0 * c1 + n
        yn = n - c1
        for m in range(8):
            h[m] = coef[m : m + 1] * h[m] + coef[16 + m : 17 + m] * (xn + coef[8 + m : 9 + m] * yn)
    last = packed_rows(kap)
    for j in range(8):
        v = jnp.where(low, seen[j], seen[j + 8])
        for p in range(16):
            msg[p, 16 * j : 16 * j + 16] = v
    for p in range(16):
        msg[p, 128:136] = last


def gather_kernel(got, own, kap, up, dn):
    low = lane_low((8, 128))

    def pair(row):
        even = got[pl.ds(row, 8, stride=272), :]
        odd = got[pl.ds(row + 136, 8, stride=272), :]
        left = jnp.where(low, even, pltpu.roll(odd, 64, 1))
        right = jnp.where(low, pltpu.roll(even, 64, 1), odd)
        return left, right

    def place(j, z, v):
        own[j, z] = v
        if j < HALO:
            if z < TRI[j]:
                dn[OFF[j] + z] = v
            if z >= 16 - TRI[j]:
                up[OFF[j] + z - (16 - TRI[j])] = v

    for j in range(8):
        for z in range(16):
            left, right = pair(16 * j + z)
            place(j, z, left)
            place(j + 8, z, right)
    for z in range(8):
        left, right = pair(128 + z)
        for at, v in ((z, left), (z + 8, right)):
            kap[at] = v
            if at < HALO:
                dn[KOFF + at] = v
            if at >= 1:
                up[KOFF + at - 1] = v


def sweep_kernel(beta, own, kown, lo, hi, parts_in, known_in, start_in, coef_in, out,
                 e, g, c, kw, parts, known, start, coef, sems):
    pairs = ((parts_in, parts), (known_in, known), (start_in, start), (coef_in, coef))
    copies = [pltpu.make_async_copy(a, b, sems.at[i]) for i, (a, b) in enumerate(pairs)]
    for copy in copies:
        copy.start()
    t = lax.axis_index("tm")
    has_lo = jnp.where(t > 0, 1.0, 0.0).astype(F32)
    has_hi = jnp.where(t < 15, 1.0, 0.0).astype(F32)

    def pick(j, first, last):
        if last <= HALO:
            start = OFF[j] + first - HALO + TRI[j]
            return has_lo * lo[start : start + last - first]
        if first > 30:
            start = OFF[j] + first - 31
            return has_hi * hi[start : start + last - first]
        return own[j, first - HALO : last - HALO]

    def groups(first, last):
        ranges = []
        for a, b in ((first, HALO), (HALO, 31), (31, last)):
            pieces = -(-(b - a) // GROUP)
            edge = [a + (b - a) * k // pieces for k in range(pieces + 1)] if pieces else []
            ranges += list(zip(edge[:-1], edge[1:]))
        return ranges

    zero = jnp.zeros((8, 128), F32)
    kw[0] = zero
    kw[47] = zero
    kw[1:16] = has_lo * lo[KOFF:MSG]
    kw[16:32] = kown[...]
    kw[32:47] = has_hi * hi[KOFF:MSG]

    lane = lax.broadcasted_iota(jnp.int32, (8, 128), 1)
    sub = lax.broadcasted_iota(jnp.int32, (8, 128), 0)
    x_start, x_end = lane < 8, lane >= 120
    y_start, y_end = lane % 8 == 0, lane % 8 == 7
    inside = (
        jnp.logical_not(x_end & (sub % 2 == 1)),
        jnp.logical_not(x_start & (sub % 2 == 0)),
        jnp.logical_not(y_end & (sub // 2 == 3)),
        jnp.logical_not(y_start & (sub // 2 == 0)),
    )

    def near(a):
        down, up = pltpu.roll(a, 8, 2), pltpu.roll(a, 120, 2)
        xm = jnp.where(x_start, pltpu.roll(down, 1, 1), down)
        xp = jnp.where(x_end, pltpu.roll(up, 7, 1), up)
        yp = pltpu.roll(jnp.where(y_start, pltpu.roll(down, 6, 1), a), 127, 2)
        ym = pltpu.roll(jnp.where(y_end, pltpu.roll(up, 2, 1), a), 1, 2)
        return xp, xm, yp, ym

    for first, last in groups(1, NEW - 1):
        kc = kw[first + 1 : last + 1]
        layer = lax.broadcasted_iota(jnp.int32, kc.shape, 0) + first
        place = t * 16 - HALO + layer
        scale = jnp.where((place >= 0) & (place < 256), 0.5 * STEP, 0.0).astype(F32)
        total = jnp.zeros_like(kc)
        for i, kn in enumerate(near(kc)):
            face = scale * (kc + jnp.where(inside[i], kn, 0.0))
            total += face
            c[i, first:last] = jnp.where(inside[i], face, 0.0)
        for i, kn in ((4, kw[first + 2 : last + 2]), (5, kw[first:last])):
            face = scale * (kc + kn)
            total += face
            c[i, first:last] = face
        c[6, first:last] = -total

    for first, last in groups(0, NEW):
        e[0, first:last] = pick(0, first, last)
    for j in range(1, 16):
        for first, last in groups(j, NEW - j):
            mid = e[j - 1, first:last]
            acc = c[6, first:last] * mid
            acc += c[4, first:last] * e[j - 1, first + 1 : last + 1]
            acc += c[5, first:last] * e[j - 1, first - 1 : last - 1]
            for d, un in enumerate(near(mid)):
                acc += c[d, first:last] * un
            for i in range(1, j):
                acc -= beta[j - 1 - i] * g[i, first:last]
            now = mid + acc + pick(j, first, last)
            g[j, first:last] = acc
            e[j, first:last] = now
    for copy in copies:
        copy.wait()
    low = lane_low((16, 128))
    p = lax.axis_index("gy") * 4 + lax.axis_index("gx")
    sublane = p // 2
    mine = low == (p % 2 == 0)
    e_rows = e.reshape(16 * LAY * 8, 128)
    g_rows = g.reshape(16 * LAY * 8, 128)

    def block_of(ref, j):
        first = (j * LAY + HALO) * 8 + sublane
        a = ref[pl.ds(first, 8, stride=8), :]
        b = ref[pl.ds(first + 64, 8, stride=8), :]
        both = jnp.concatenate([a, b], axis=0)
        return jnp.where(mine, both, pltpu.roll(both, 64, 1))

    h = [start[16 * m : 16 * m + 16] for m in range(8)]
    for j in range(16):
        c1, c2 = doubled(parts[j, 0:16], low)
        n = known[j]
        if j > 0:
            n = n + block_of(g_rows, j)
        xn = c2 - 2.0 * c1 + n
        yn = n - c1
        for m in range(8):
            h[m] = coef[m : m + 1] * h[m] + coef[16 + m : 17 + m] * (xn + coef[8 + m : 9 + m] * yn)
            if j % 2 == 0:
                at_row = 16 * (m % 4)
                out[j + m // 4, at_row : at_row + 16] = h[m]
        out[j, 64:72] = packed_rows(block_of(e_rows, j))


def rows_of(ref):
    return jnp.concatenate([unpacked(ref[t, 64:72]) for t in range(16)], axis=0)


def field_kernel(got, fine, field, part):
    now = rows_of(got).T[0:64]
    field[...] = now
    diff = now - fine[...]
    diff = diff * diff
    total = jnp.zeros((8, 128), F32)
    for x in range(8):
        total += diff[8 * x : 8 * x + 8, 0:128] + diff[8 * x : 8 * x + 8, 128:256]
    for p in range(16):
        part[p] = total


def final_kernel(got, other, mine, coef, modes):
    def finish(low, high, odd):
        x = y = None
        if odd:
            c1, c2 = doubled(mine[:, 0:16].reshape(256, 128), lane_low((256, 128)))
            x = rows_of(high) - rows_of(low) - c1
            y = x - c2 + c1
        for m in range(8):
            src = low if m < 4 else high
            first = 16 * (m % 4)
            both = src[:, first : first + 16].reshape(256, 128)
            if odd:
                both = coef[m : m + 1] * both
                both += coef[16 + m : 17 + m] * (x + coef[8 + m : 9 + m] * y)
            both = both.T
            modes[m] = both[0:64]
            modes[m + 8] = both[64:128]

    t = lax.axis_index("tm")

    @pl.when(t % 2 == 0)
    def _():
        finish(got, other, False)

    @pl.when(t % 2 == 1)
    def _():
        finish(other, got, True)


def ring(axis, step):
    n = lax.axis_size(axis)
    return [(i, (i + step) % n) for i in range(n)]


def swap(value, axis):
    return lax.all_to_all(value, axis, 0, 0, tiled=True)


def per_device(field, modes, source, regions, region_kappa, mode_rate, mode_weight):
    u = field.reshape(64, 256)
    h = modes.reshape(16, 64, 256)
    s = source.reshape(64, 256)
    reg = regions.reshape(64, 256)
    t = lax.axis_index("tm")

    f = jnp.exp(-0.5 * mode_rate)
    e = jnp.exp(-mode_rate)
    w = mode_weight
    omega = jnp.sum(w * (1.0 - f)).reshape(1)
    powers = jnp.exp(-mode_rate[None, :] * jnp.arange(16, dtype=F32)[:, None])
    beta = STEP * jnp.sum((w * (1.0 - e))[None, :] * powers, axis=1)
    coef = jnp.concatenate([e, f, 1.0 - f, w]).reshape(4, 2, 8).transpose(0, 2, 1)
    coef = jnp.broadcast_to(coef[..., None], (4, 8, 2, 64)).reshape(32, 128)

    plane = (64, 256)
    outs = [plane] * 4 + [(40, 256)] * 2 + [(256, 128)]
    u, kap, g0, q1s, up, dn, sk = pl.pallas_call(
        local_kernel,
        out_shape=[jax.ShapeDtypeStruct(shape, F32) for shape in outs],
        in_specs=[ANY] * 7,
        out_specs=[VM] * 7,
        scratch_shapes=[pltpu.SMEM((8,), F32), pltpu.SMEM((16,), F32), pltpu.SMEM((16,), F32)]
        + [pltpu.VMEM(plane, jnp.int32), pltpu.VMEM(plane, F32), pltpu.VMEM((16, 64, 256), F32)]
        + [pltpu.SemaphoreType.DMA((10,))],
        compiler_params=pltpu.CompilerParams(vmem_limit_bytes=60 * MIB),
    )(region_kappa, w, mode_rate, u, reg, s, h)
    xlo = lax.ppermute(up, "gx", ring("gx", 1))
    xhi = lax.ppermute(dn, "gx", ring("gx", -1))
    chunks = pl.pallas_call(
        scatter_kernel,
        out_shape=[jax.ShapeDtypeStruct((6, 128, 128), F32)] * 3,
        in_specs=[ANY, ANY],
        out_specs=[ANY] * 3,
        scratch_shapes=[pltpu.VMEM((16, 64, 256), F32), pltpu.VMEM((18, 128, 128), F32)]
        + [pltpu.SemaphoreType.DMA((7,))],
        compiler_params=pltpu.CompilerParams(vmem_limit_bytes=60 * MIB),
    )(sk, h)

    yup, ydn = call(side_kernel, [(80, 256)] * 2, 5, 0)(u, kap, g0, xlo, xhi)
    ylo = lax.ppermute(yup, "gy", ring("gy", 1))
    yhi = lax.ppermute(ydn, "gy", ring("gy", -1))
    far = [lax.ppermute(chunks[k], "tm", [(0, hub)]) for k, hub in ((1, 4), (2, 12))]

    fine, both = call(
        fine_kernel, [plane, (16, 24, 128)], 9, 1, [(12, 24, 256)] * 4, 16, LONG
    )(omega, u, kap, g0, q1s, xlo, xhi, ylo, yhi)
    parts = swap(both, "tm")

    share = jnp.where(t == 0, chunks[0], far[0] + far[1])
    pairs = [[(0, k), (4, 4 + k), (12, 12 + k)] for k in (1, 2, 3)]
    pairs += [[(4, 8), (12, 11)], [(4, 9), (12, 10)]]
    close = [lax.ppermute(share[k + 1], "tm", pair) for k, pair in enumerate(pairs)]
    hub = (t == 0) | (t == 4) | (t == 12)
    start = jnp.where(hub, share[0], sum(close))

    msg, known = call(known_kernel, [(16, 136, 128), (16, 16, 128)], 4, 0)(
        parts, sk, start, coef
    )
    got = swap(msg, ("gy", "gx"))
    own, kown, up, dn = call(
        gather_kernel, [(16, 16, 8, 128), (16, 8, 128), (MSG, 8, 128), (MSG, 8, 128)], 1, 0
    )(got.reshape(16 * 136, 128))
    lo = lax.ppermute(up, "tm", ring("tm", 1))
    hi = lax.ppermute(dn, "tm", ring("tm", -1))
    out = pl.pallas_call(
        sweep_kernel,
        out_shape=jax.ShapeDtypeStruct((16, 72, 128), F32),
        in_specs=[SM] + [VM] * 4 + [ANY] * 4,
        out_specs=VM,
        scratch_shapes=[
            pltpu.VMEM(shape, F32)
            for shape in (
                (16, LAY, 8, 128),
                (16, LAY, 8, 128),
                (7, LAY, 8, 128),
                (LAY, 8, 128),
                (16, 24, 128),
                (16, 16, 128),
                (128, 128),
                (32, 128),
            )
        ]
        + [pltpu.SemaphoreType.DMA((4,))],
        compiler_params=pltpu.CompilerParams(vmem_limit_bytes=24 * MIB),
    )(beta, own, kown, lo, hi, parts, known, start, coef)
    back = swap(out, "tm")
    other = lax.ppermute(back, "tm", [(i, i ^ 1) for i in range(16)])
    new_field, part = call(field_kernel, [plane, (16, 8, 128)], 2, 0)(back, fine)
    parted = swap(part, ("gy", "gx"))
    new_modes = call(final_kernel, [(16, 64, 256)], 4, 0)(back, other, both, coef)[0]
    parted, new_modes = lax.optimization_barrier((parted, new_modes))
    size = jnp.sqrt(jnp.sum(parted) / 262144.0).reshape(1)
    return (new_field.reshape(1, 8, 8, 256), new_modes.reshape(1, 16, 8, 8, 256), size)


def solution(mesh):
    return jax.shard_map(
        per_device,
        mesh=mesh,
        in_specs=(
            P("tm", "gx", "gy", None),
            P("tm", None, "gx", "gy", None),
            P("gx", "gy", None),
            P("gx", "gy", None),
            P(),
            P(),
            P(),
        ),
        out_specs=(P("tm", "gx", "gy", None), P("tm", None, "gx", "gy", None), P("tm")),
        check_vma=False,
    )
```

```python
import functools
import jax
import jax.numpy as jnp
from jax import lax
from jax.experimental import pallas as pl
from jax.experimental.pallas import tpu as pltpu
from jax.sharding import PartitionSpec as P

STEP = 0.12
F32 = jnp.float32
VM = pl.BlockSpec(memory_space=pltpu.VMEM)
SM = pl.BlockSpec(memory_space=pltpu.SMEM)
ANY = pl.BlockSpec(memory_space=pl.ANY)
MIB = 1024 * 1024
LONG = pl.CostEstimate(flops=20_000_000_000, bytes_accessed=1_000_000, transcendentals=0)
SLOTS = [0, 1, 2, 3, 0, 0, 4, 5, 6, 7, 8, 9, 12, 13, 14, 15, 11, 10]
HALO = 15
TRI = [HALO] + [HALO - j for j in range(1, HALO)]
OFF = [sum(TRI[:j]) for j in range(HALO)]
KOFF = sum(TRI)
MSG = KOFF + HALO
LAY = 48
NEW = 46
GROUP = 16


def call(kernel, outs, ins, smem, scratch=(), limit=16, cost=None):
    return pl.pallas_call(
        kernel,
        out_shape=[jax.ShapeDtypeStruct(shape, F32) for shape in outs],
        in_specs=[SM] * smem + [VM] * (ins - smem),
        out_specs=[VM] * len(outs),
        scratch_shapes=[pltpu.VMEM(shape, F32) for shape in scratch],
        compiler_params=pltpu.CompilerParams(vmem_limit_bytes=limit * MIB),
        cost_estimate=cost,
    )


def lane_low(shape):
    return lax.broadcasted_iota(jnp.int32, shape, len(shape) - 1) < 64


def local_kernel(rk_in, w_in, rate_in, u_in, reg_in, s_in, modes_in, u, kap, g0, q1s, up, dn, sk,
                 rk, w, rate, reg, s, modes, sems):
    pairs = [(u_in, u), (reg_in, reg), (s_in, s), (rk_in, rk), (w_in, w), (rate_in, rate)]
    pairs += [(modes_in.at[pl.ds(4 * i, 4)], modes.at[pl.ds(4 * i, 4)]) for i in range(4)]
    copies = [pltpu.make_async_copy(a, b, sems.at[i]) for i, (a, b) in enumerate(pairs)]
    for copy in copies:
        copy.start()
    for copy in copies[:6]:
        copy.wait()
    for x in range(8):
        rows = slice(8 * x, 8 * x + 8)
        region = reg[rows]
        k = jnp.zeros((8, 256), F32)
        for r in range(8):
            k = jnp.where(region == r, rk[r], k)
        kap[rows] = k
    half = [jnp.exp(jnp.full((8, 256), -0.5 * rate[m], F32)) for m in range(16)]
    a = [s[8 * x : 8 * x + 8] for x in range(8)]
    b = [s[8 * x : 8 * x + 8] for x in range(8)]
    for m in range(16):
        if m % 4 == 0:
            copies[6 + m // 4].wait()
        for x in range(8):
            h = w[m] * modes[m, 8 * x : 8 * x + 8]
            a[x] = a[x] - h
            b[x] = b[x] - half[m] * h
    for x in range(8):
        g0[8 * x : 8 * x + 8] = a[x]
        q1s[8 * x : 8 * x + 8] = b[x]
    up[0:16] = u[48:64]
    up[16:32] = kap[48:64]
    up[32:40] = g0[56:64]
    dn[0:16] = u[0:16]
    dn[16:32] = kap[0:16]
    dn[32:40] = g0[0:8]
    sk[...] = jnp.concatenate([s[...], kap[...]], axis=0).T


def scatter_kernel(after, modes_in, out0, out1, out2, modes, packed, sems):
    @pl.when(lax.axis_index("tm") == 0)
    def _():
        copies = [
            pltpu.make_async_copy(modes_in.at[pl.ds(4 * i, 4)], modes.at[pl.ds(4 * i, 4)], sems.at[i])
            for i in range(4)
        ]
        for copy in copies:
            copy.start()
        for copy in copies:
            copy.wait()
        for m in range(8):
            both = jnp.concatenate([modes[m], modes[m + 8]], axis=0).T
            pieces = both.reshape(16, 16, 128)
            for place, slot in enumerate(SLOTS):
                packed[place, 16 * m : 16 * m + 16] = pieces[slot]
        copies = [
            pltpu.make_async_copy(packed.at[pl.ds(6 * i, 6)], out, sems.at[4 + i])
            for i, out in enumerate((out0, out1, out2))
        ]
        for copy in copies:
            copy.start()
        for copy in copies:
            copy.wait()


def side_kernel(u, kap, g0, xlo, xhi, yup, ydn):
    has_lo = jnp.where(lax.axis_index("gx") > 0, 1.0, 0.0).astype(F32)
    has_hi = jnp.where(lax.axis_index("gx") < 3, 1.0, 0.0).astype(F32)
    for out, first in ((yup, 6), (ydn, 0)):
        for piece in range(5):
            if piece < 4:
                src, base = (u, 0) if piece < 2 else (kap, 16)
                y = first + piece % 2
                out[16 * piece : 16 * piece + 1] = has_lo * xlo[base + 8 + y : base + 9 + y]
                out[16 * piece + 9 : 16 * piece + 10] = has_hi * xhi[base + y : base + y + 1]
            else:
                src = g0
                y = 7 if first else 0
            for x in range(8):
                at_row = 16 * piece + 1 + x
                out[at_row : at_row + 1] = src[8 * x + y : 8 * x + y + 1]


def fine_kernel(omega, u, kap, g0, q1s, xlo, xhi, ylo, yhi, both, up, kp, gp, u1):
    gx, gy = lax.axis_index("gx"), lax.axis_index("gy")
    zero = jnp.zeros((24, 256), F32)
    for ref in (up, kp, gp):
        for x in range(12):
            ref[x] = zero
    for x in range(8):
        rows = slice(8 * x, 8 * x + 8)
        up[2 + x, 8:16] = u[rows]
        kp[2 + x, 8:16] = kap[rows]
        gp[2 + x, 8:16] = g0[rows]

    @pl.when(gx > 0)
    def _():
        for i in range(2):
            up[i, 8:16] = xlo[8 * i : 8 * i + 8]
            kp[i, 8:16] = xlo[16 + 8 * i : 24 + 8 * i]
        gp[1, 8:16] = xlo[32:40]

    @pl.when(gx < 3)
    def _():
        for i in range(2):
            up[10 + i, 8:16] = xhi[8 * i : 8 * i + 8]
            kp[10 + i, 8:16] = xhi[16 + 8 * i : 24 + 8 * i]
        gp[10, 8:16] = xhi[32:40]

    for cond, ref, row in ((gy > 0, ylo, 6), (gy < 3, yhi, 16)):

        @pl.when(cond)
        def _(ref=ref, row=row):
            for x in range(10):
                for i in range(2):
                    up[1 + x, row + i : row + i + 1] = ref[16 * i + x : 16 * i + x + 1]
                    kp[1 + x, row + i : row + i + 1] = ref[32 + 16 * i + x : 33 + 16 * i + x]
                if 1 <= x <= 8:
                    near = 7 if row == 6 else 16
                    gp[1 + x, near : near + 1] = ref[64 + x : 65 + x]

    z = lax.broadcasted_iota(jnp.int32, (24, 256), 1)

    def above(v):
        return jnp.where(z == 255, 0.0, pltpu.roll(v, 255, 1))

    def below(v):
        return jnp.where(z == 0, 0.0, pltpu.roll(v, 1, 1))

    def laplace(ref, x):
        uc, kc = ref[x], kp[x]
        total = jnp.zeros((24, 256), F32)
        for near_u, near_k in (
            (ref[x + 1], kp[x + 1]),
            (ref[x - 1], kp[x - 1]),
            (pltpu.roll(uc, 23, 0), pltpu.roll(kc, 23, 0)),
            (pltpu.roll(uc, 1, 0), pltpu.roll(kc, 1, 0)),
            (above(uc), above(kc)),
            (below(uc), below(kc)),
        ):
            total += (kc + near_k) * (near_u - uc)
        return 0.5 * total

    for x in range(1, 11):
        change = (0.5 * STEP) * (laplace(up, x) + gp[x])
        u1[x] = up[x] + change
        gp[x] = change

    @pl.when(gx == 0)
    def _():
        u1[1] = zero

    @pl.when(gx == 3)
    def _():
        u1[10] = zero

    @pl.when(gy == 0)
    def _():
        for x in range(1, 11):
            u1[x, 0:8] = zero[0:8]

    @pl.when(gy == 3)
    def _():
        for x in range(1, 11):
            u1[x, 16:24] = zero[0:8]

    first, second = [], []
    for x in range(8):
        rows = slice(8 * x, 8 * x + 8)
        c1 = gp[2 + x, 8:16]
        lap = laplace(u1, 2 + x)[8:16]
        c2 = (0.5 * STEP) * (lap + q1s[rows] - omega[0] * c1)
        first.append(c1)
        second.append(c2)
    both[:, 0:16] = jnp.concatenate(first + second, axis=0).T.reshape(16, 16, 128)
    now = jnp.concatenate([u[...], u[...]], axis=0).T.reshape(16, 16, 128)
    both[:, 16:24] = jnp.where(lane_low((16, 8, 128)), now[:, 0:8], now[:, 8:16])


def doubled(v, low):
    turned = pltpu.roll(v, 64, 1)
    return jnp.where(low, v, turned), jnp.where(low, turned, v)


def unpacked(v):
    low = lane_low((8, 128))
    first, second = doubled(v, low)
    return jnp.concatenate([first, second], axis=0)


def packed_rows(v):
    return jnp.where(lane_low((8, 128)), v[0:8], v[8:16])


def known_kernel(parts, sk, start, coef, msg, known):
    low = lane_low((16, 128))
    slab = sk[pl.ds(pl.multiple_of(lax.axis_index("tm") * 16, 16), 16), :]
    source, kap = doubled(slab, low)
    h = [start[16 * m : 16 * m + 16] for m in range(8)]
    seen = []
    for j in range(16):
        c1, c2 = doubled(parts[j, 0:16], low)
        msg[j, 136:144] = packed_rows(unpacked(parts[j, 16:24]) + c1 + c2)
        if j == 0:
            n = 2.0 * c1
            seen.append(unpacked(parts[0, 16:24]) + c1 + c2)
        else:
            q = coef[24:25] * h[0]
            for m in range(1, 8):
                q += coef[24 + m : 25 + m] * h[m]
            n = STEP * (source - (q + pltpu.roll(q, 64, 1)))
            seen.append(n + c2 - c1)
        known[j] = n
        xn = c2 - 2.0 * c1 + n
        yn = n - c1
        for m in range(8):
            h[m] = coef[m : m + 1] * h[m] + coef[16 + m : 17 + m] * (xn + coef[8 + m : 9 + m] * yn)
    last = packed_rows(kap)
    for j in range(8):
        v = jnp.where(low, seen[j], seen[j + 8])
        for p in range(16):
            msg[p, 16 * j : 16 * j + 16] = v
    for p in range(16):
        msg[p, 128:136] = last


def gather_kernel(got, own, kap, fine, up, dn):
    low = lane_low((8, 128))

    def pair(row):
        even = got[pl.ds(row, 8, stride=288), :]
        odd = got[pl.ds(row + 144, 8, stride=288), :]
        left = jnp.where(low, even, pltpu.roll(odd, 64, 1))
        right = jnp.where(low, pltpu.roll(even, 64, 1), odd)
        return left, right

    def place(j, z, v):
        own[j, z] = v
        if j < HALO:
            if z < TRI[j]:
                dn[OFF[j] + z] = v
            if z >= 16 - TRI[j]:
                up[OFF[j] + z - (16 - TRI[j])] = v

    for j in range(8):
        for z in range(16):
            left, right = pair(16 * j + z)
            place(j, z, left)
            place(j + 8, z, right)
    for z in range(8):
        fine[z], fine[z + 8] = pair(136 + z)
        left, right = pair(128 + z)
        for at, v in ((z, left), (z + 8, right)):
            kap[at] = v
            if at < HALO:
                dn[KOFF + at] = v
            if at >= 1:
                up[KOFF + at - 1] = v


def sweep_kernel(beta, own, kown, fown, lo, hi, parts_in, known_in, start_in, coef_in, out,
                 e, g, c, kw, parts, known, start, coef, sems):
    pairs = ((parts_in, parts), (known_in, known), (start_in, start), (coef_in, coef))
    copies = [pltpu.make_async_copy(a, b, sems.at[i]) for i, (a, b) in enumerate(pairs)]
    for copy in copies:
        copy.start()
    t = lax.axis_index("tm")
    has_lo = jnp.where(t > 0, 1.0, 0.0).astype(F32)
    has_hi = jnp.where(t < 15, 1.0, 0.0).astype(F32)

    def pick(j, first, last):
        if last <= HALO:
            start = OFF[j] + first - HALO + TRI[j]
            return has_lo * lo[start : start + last - first]
        if first > 30:
            start = OFF[j] + first - 31
            return has_hi * hi[start : start + last - first]
        return own[j, first - HALO : last - HALO]

    def groups(first, last):
        ranges = []
        for a, b in ((first, HALO), (HALO, 31), (31, last)):
            pieces = -(-(b - a) // GROUP)
            edge = [a + (b - a) * k // pieces for k in range(pieces + 1)] if pieces else []
            ranges += list(zip(edge[:-1], edge[1:]))
        return ranges

    zero = jnp.zeros((8, 128), F32)
    kw[0] = zero
    kw[47] = zero
    kw[1:16] = has_lo * lo[KOFF:MSG]
    kw[16:32] = kown[...]
    kw[32:47] = has_hi * hi[KOFF:MSG]

    lane = lax.broadcasted_iota(jnp.int32, (8, 128), 1)
    sub = lax.broadcasted_iota(jnp.int32, (8, 128), 0)
    x_start, x_end = lane < 8, lane >= 120
    y_start, y_end = lane % 8 == 0, lane % 8 == 7
    inside = (
        jnp.logical_not(x_end & (sub % 2 == 1)),
        jnp.logical_not(x_start & (sub % 2 == 0)),
        jnp.logical_not(y_end & (sub // 2 == 3)),
        jnp.logical_not(y_start & (sub // 2 == 0)),
    )

    def near(a):
        down, up = pltpu.roll(a, 8, 2), pltpu.roll(a, 120, 2)
        xm = jnp.where(x_start, pltpu.roll(down, 1, 1), down)
        xp = jnp.where(x_end, pltpu.roll(up, 7, 1), up)
        yp = pltpu.roll(jnp.where(y_start, pltpu.roll(down, 6, 1), a), 127, 2)
        ym = pltpu.roll(jnp.where(y_end, pltpu.roll(up, 2, 1), a), 1, 2)
        return xp, xm, yp, ym

    for first, last in groups(1, NEW - 1):
        kc = kw[first + 1 : last + 1]
        layer = lax.broadcasted_iota(jnp.int32, kc.shape, 0) + first
        place = t * 16 - HALO + layer
        scale = jnp.where((place >= 0) & (place < 256), 0.5 * STEP, 0.0).astype(F32)
        total = jnp.zeros_like(kc)
        for i, kn in enumerate(near(kc)):
            face = scale * (kc + jnp.where(inside[i], kn, 0.0))
            total += face
            c[i, first:last] = jnp.where(inside[i], face, 0.0)
        for i, kn in ((4, kw[first + 2 : last + 2]), (5, kw[first:last])):
            face = scale * (kc + kn)
            total += face
            c[i, first:last] = face
        c[6, first:last] = -total

    for first, last in groups(0, NEW):
        e[0, first:last] = pick(0, first, last)
    for j in range(1, 16):
        for first, last in groups(j, NEW - j):
            mid = e[j - 1, first:last]
            acc = c[6, first:last] * mid
            acc += c[4, first:last] * e[j - 1, first + 1 : last + 1]
            acc += c[5, first:last] * e[j - 1, first - 1 : last - 1]
            for d, un in enumerate(near(mid)):
                acc += c[d, first:last] * un
            for i in range(1, j):
                acc -= beta[j - 1 - i] * g[i, first:last]
            now = mid + acc + pick(j, first, last)
            g[j, first:last] = acc
            e[j, first:last] = now
    for copy in copies:
        copy.wait()
    low = lane_low((16, 128))
    p = lax.axis_index("gy") * 4 + lax.axis_index("gx")
    sublane = p // 2
    mine = low == (p % 2 == 0)
    e_rows = e.reshape(16 * LAY * 8, 128)
    g_rows = g.reshape(16 * LAY * 8, 128)

    def block_of(ref, j):
        first = (j * LAY + HALO) * 8 + sublane
        a = ref[pl.ds(first, 8, stride=8), :]
        b = ref[pl.ds(first + 64, 8, stride=8), :]
        both = jnp.concatenate([a, b], axis=0)
        return jnp.where(mine, both, pltpu.roll(both, 64, 1))

    h = [start[16 * m : 16 * m + 16] for m in range(8)]
    for j in range(16):
        c1, c2 = doubled(parts[j, 0:16], low)
        n = known[j]
        if j > 0:
            n = n + block_of(g_rows, j)
        xn = c2 - 2.0 * c1 + n
        yn = n - c1
        for m in range(8):
            h[m] = coef[m : m + 1] * h[m] + coef[16 + m : 17 + m] * (xn + coef[8 + m : 9 + m] * yn)
            if j % 2 == 0:
                at_row = 16 * (m % 4)
                out[j + m // 4, at_row : at_row + 16] = h[m]
        out[j, 64:72] = packed_rows(block_of(e_rows, j))
    diff = e[p, HALO:31] - fown[...]
    part = jnp.sum(diff * diff, axis=0)
    for j in range(16):
        out[j, 72:80] = part


def rows_of(ref):
    return jnp.concatenate([unpacked(ref[t, 64:72]) for t in range(16)], axis=0)


def field_kernel(got, field, size):
    field[...] = rows_of(got).T[0:64]
    part = got[0, 72:80]
    for t in range(1, 16):
        part += got[t, 72:80]
    whole = jnp.sum(jnp.sum(part, axis=1, keepdims=True), axis=0, keepdims=True)
    size[0] = jnp.sqrt(whole / 262144.0)[0, 0]


def final_kernel(got, other, mine, coef, modes):
    def finish(low, high, odd):
        x = y = None
        if odd:
            c1, c2 = doubled(mine[:, 0:16].reshape(256, 128), lane_low((256, 128)))
            x = rows_of(high) - rows_of(low) - c1
            y = x - c2 + c1
        for m in range(8):
            src = low if m < 4 else high
            first = 16 * (m % 4)
            both = src[:, first : first + 16].reshape(256, 128)
            if odd:
                both = coef[m : m + 1] * both
                both += coef[16 + m : 17 + m] * (x + coef[8 + m : 9 + m] * y)
            both = both.T
            modes[m] = both[0:64]
            modes[m + 8] = both[64:128]

    t = lax.axis_index("tm")

    @pl.when(t % 2 == 0)
    def _():
        finish(got, other, False)

    @pl.when(t % 2 == 1)
    def _():
        finish(other, got, True)


def ring(axis, step):
    n = lax.axis_size(axis)
    return [(i, (i + step) % n) for i in range(n)]


def turned():
    def apart(a, b, n):
        return min((a - b) % n, (b - a) % n)

    def device(t, p):
        return 16 * t + p % 4 * 4 + p // 4

    pairs = []
    for j in range(16):
        far = sorted(range(16), key=lambda p: -apart(p % 4, j % 4, 4) - apart(p // 4, j // 4, 4))
        near = sorted(range(16), key=lambda t: apart(t // 2, j // 2, 8))
        pairs += [(device(t, j), device(j, p)) for t, p in zip(near, far)]
    return pairs


def swap(value, axis):
    return lax.all_to_all(value, axis, 0, 0, tiled=True)


def per_device(field, modes, source, regions, region_kappa, mode_rate, mode_weight):
    u = field.reshape(64, 256)
    h = modes.reshape(16, 64, 256)
    s = source.reshape(64, 256)
    reg = regions.reshape(64, 256)
    t = lax.axis_index("tm")

    f = jnp.exp(-0.5 * mode_rate)
    e = jnp.exp(-mode_rate)
    w = mode_weight
    omega = jnp.sum(w * (1.0 - f)).reshape(1)
    powers = jnp.exp(-mode_rate[None, :] * jnp.arange(16, dtype=F32)[:, None])
    beta = STEP * jnp.sum((w * (1.0 - e))[None, :] * powers, axis=1)
    coef = jnp.concatenate([e, f, 1.0 - f, w]).reshape(4, 2, 8).transpose(0, 2, 1)
    coef = jnp.broadcast_to(coef[..., None], (4, 8, 2, 64)).reshape(32, 128)

    plane = (64, 256)
    outs = [plane] * 4 + [(40, 256)] * 2 + [(256, 128)]
    u, kap, g0, q1s, up, dn, sk = pl.pallas_call(
        local_kernel,
        out_shape=[jax.ShapeDtypeStruct(shape, F32) for shape in outs],
        in_specs=[ANY] * 7,
        out_specs=[VM] * 7,
        scratch_shapes=[pltpu.SMEM((8,), F32), pltpu.SMEM((16,), F32), pltpu.SMEM((16,), F32)]
        + [pltpu.VMEM(plane, jnp.int32), pltpu.VMEM(plane, F32), pltpu.VMEM((16, 64, 256), F32)]
        + [pltpu.SemaphoreType.DMA((10,))],
        compiler_params=pltpu.CompilerParams(vmem_limit_bytes=60 * MIB),
    )(region_kappa, w, mode_rate, u, reg, s, h)
    xlo = lax.ppermute(up, "gx", ring("gx", 1))
    xhi = lax.ppermute(dn, "gx", ring("gx", -1))
    chunks = pl.pallas_call(
        scatter_kernel,
        out_shape=[jax.ShapeDtypeStruct((6, 128, 128), F32)] * 3,
        in_specs=[ANY, ANY],
        out_specs=[ANY] * 3,
        scratch_shapes=[pltpu.VMEM((16, 64, 256), F32), pltpu.VMEM((18, 128, 128), F32)]
        + [pltpu.SemaphoreType.DMA((7,))],
        compiler_params=pltpu.CompilerParams(vmem_limit_bytes=60 * MIB),
    )(sk, h)

    yup, ydn = call(side_kernel, [(80, 256)] * 2, 5, 0)(u, kap, g0, xlo, xhi)
    ylo = lax.ppermute(yup, "gy", ring("gy", 1))
    yhi = lax.ppermute(ydn, "gy", ring("gy", -1))
    far = [lax.ppermute(chunks[k], "tm", [(0, hub)]) for k, hub in ((1, 4), (2, 12))]

    (both,) = call(
        fine_kernel, [(16, 24, 128)], 9, 1, [(12, 24, 256)] * 4, 16, LONG
    )(omega, u, kap, g0, q1s, xlo, xhi, ylo, yhi)
    parts = swap(both, "tm")

    share = jnp.where(t == 0, chunks[0], far[0] + far[1])
    pairs = [[(0, k), (4, 4 + k), (12, 12 + k)] for k in (1, 2, 3)]
    pairs += [[(4, 8), (12, 11)], [(4, 9), (12, 10)]]
    close = [lax.ppermute(share[k + 1], "tm", pair) for k, pair in enumerate(pairs)]
    hub = (t == 0) | (t == 4) | (t == 12)
    start = jnp.where(hub, share[0], sum(close))

    msg, known = call(known_kernel, [(16, 144, 128), (16, 16, 128)], 4, 0)(
        parts, sk, start, coef
    )
    got = swap(msg, ("gy", "gx"))
    own, kown, fown, up, dn = call(
        gather_kernel,
        [(16, 16, 8, 128), (16, 8, 128), (16, 8, 128), (MSG, 8, 128), (MSG, 8, 128)],
        1,
        0,
    )(got.reshape(16 * 144, 128))
    lo = lax.ppermute(up, "tm", ring("tm", 1))
    hi = lax.ppermute(dn, "tm", ring("tm", -1))
    out = pl.pallas_call(
        sweep_kernel,
        out_shape=jax.ShapeDtypeStruct((16, 80, 128), F32),
        in_specs=[SM] + [VM] * 5 + [ANY] * 4,
        out_specs=VM,
        scratch_shapes=[
            pltpu.VMEM(shape, F32)
            for shape in (
                (16, LAY, 8, 128),
                (16, LAY, 8, 128),
                (7, LAY, 8, 128),
                (LAY, 8, 128),
                (16, 24, 128),
                (16, 16, 128),
                (128, 128),
                (32, 128),
            )
        ]
        + [pltpu.SemaphoreType.DMA((4,))],
        compiler_params=pltpu.CompilerParams(vmem_limit_bytes=24 * MIB),
    )(beta, own, kown, fown, lo, hi, parts, known, start, coef)
    back = swap(out, "tm")
    other = lax.ppermute(back, "tm", [(i, i ^ 1) for i in range(16)])
    new_field, size = pl.pallas_call(
        field_kernel,
        out_shape=[jax.ShapeDtypeStruct(shape, F32) for shape in (plane, (1,))],
        in_specs=[VM],
        out_specs=[VM, SM],
        compiler_params=pltpu.CompilerParams(vmem_limit_bytes=16 * MIB),
    )(back)
    size = lax.ppermute(size, ("tm", "gx", "gy"), turned())
    new_modes = call(final_kernel, [(16, 64, 256)], 4, 0)(back, other, both, coef)[0]
    size, new_modes = lax.optimization_barrier((size, new_modes))
    return (new_field.reshape(1, 8, 8, 256), new_modes.reshape(1, 16, 8, 8, 256), size)


def solution(mesh):
    return jax.shard_map(
        per_device,
        mesh=mesh,
        in_specs=(
            P("tm", "gx", "gy", None),
            P("tm", None, "gx", "gy", None),
            P("gx", "gy", None),
            P("gx", "gy", None),
            P(),
            P(),
            P(),
        ),
        out_specs=(P("tm", "gx", "gy", None), P("tm", None, "gx", "gy", None), P("tm")),
        check_vma=False,
    )
```

```python
import functools
import jax
import jax.numpy as jnp
from jax import lax
from jax.experimental import pallas as pl
from jax.experimental.pallas import tpu as pltpu
from jax.sharding import PartitionSpec as P

STEP = 0.12
F32 = jnp.float32
VM = pl.BlockSpec(memory_space=pltpu.VMEM)
SM = pl.BlockSpec(memory_space=pltpu.SMEM)
ANY = pl.BlockSpec(memory_space=pl.ANY)
MIB = 1024 * 1024
LONG = pl.CostEstimate(flops=20_000_000_000, bytes_accessed=1_000_000, transcendentals=0)
HALO = 15
TRI = [HALO] + [HALO - j for j in range(1, HALO)]
OFF = [sum(TRI[:j]) for j in range(HALO)]
KOFF = sum(TRI)
MSG = KOFF + HALO
LAY = 48
NEW = 46
GROUP = 16


def call(kernel, outs, ins, smem, scratch=(), limit=16, cost=None):
    return pl.pallas_call(
        kernel,
        out_shape=[jax.ShapeDtypeStruct(shape, F32) for shape in outs],
        in_specs=[SM] * smem + [VM] * (ins - smem),
        out_specs=[VM] * len(outs),
        scratch_shapes=[pltpu.VMEM(shape, F32) for shape in scratch],
        compiler_params=pltpu.CompilerParams(vmem_limit_bytes=limit * MIB),
        cost_estimate=cost,
    )


def lane_low(shape):
    return lax.broadcasted_iota(jnp.int32, shape, len(shape) - 1) < 64


def local_kernel(rk_in, w_in, rate_in, u_in, reg_in, s_in, modes_in, u, kap, g0, q1s, up, dn, sk,
                 rk, w, rate, reg, s, modes, sems):
    pairs = [(u_in, u), (reg_in, reg), (s_in, s), (rk_in, rk), (w_in, w), (rate_in, rate)]
    pairs += [(modes_in.at[pl.ds(4 * i, 4)], modes.at[pl.ds(4 * i, 4)]) for i in range(4)]
    copies = [pltpu.make_async_copy(a, b, sems.at[i]) for i, (a, b) in enumerate(pairs)]
    for copy in copies:
        copy.start()
    for copy in copies[:6]:
        copy.wait()
    for x in range(8):
        rows = slice(8 * x, 8 * x + 8)
        region = reg[rows]
        k = jnp.zeros((8, 256), F32)
        for r in range(8):
            k = jnp.where(region == r, rk[r], k)
        kap[rows] = k
    half = [jnp.exp(jnp.full((8, 256), -0.5 * rate[m], F32)) for m in range(16)]
    a = [s[8 * x : 8 * x + 8] for x in range(8)]
    b = [s[8 * x : 8 * x + 8] for x in range(8)]
    for m in range(16):
        if m % 4 == 0:
            copies[6 + m // 4].wait()
        for x in range(8):
            h = w[m] * modes[m, 8 * x : 8 * x + 8]
            a[x] = a[x] - h
            b[x] = b[x] - half[m] * h
    for x in range(8):
        g0[8 * x : 8 * x + 8] = a[x]
        q1s[8 * x : 8 * x + 8] = b[x]
    up[0:16] = u[48:64]
    up[16:32] = kap[48:64]
    up[32:40] = g0[56:64]
    dn[0:16] = u[0:16]
    dn[16:32] = kap[0:16]
    dn[32:40] = g0[0:8]
    sk[...] = jnp.concatenate([s[...], kap[...]], axis=0).T


def scatter_kernel(after, modes_in, out0, out1, out2, out3, modes, packed, sems):
    @pl.when(lax.axis_index("tm") == 0)
    def _():
        copies = [
            pltpu.make_async_copy(modes_in.at[pl.ds(4 * i, 4)], modes.at[pl.ds(4 * i, 4)], sems.at[i])
            for i in range(4)
        ]
        for copy in copies:
            copy.start()
        for copy in copies:
            copy.wait()
        for m in range(8):
            both = jnp.concatenate([modes[m], modes[m + 8]], axis=0).T
            packed[:, 16 * m : 16 * m + 16] = both.reshape(16, 16, 128)
        copies = [
            pltpu.make_async_copy(packed.at[pl.ds(4 * i, 4)], out, sems.at[4 + i])
            for i, out in enumerate((out0, out1, out2, out3))
        ]
        for copy in copies:
            copy.start()
        for copy in copies:
            copy.wait()


def side_kernel(u, kap, g0, xlo, xhi, yup, ydn):
    has_lo = jnp.where(lax.axis_index("gx") > 0, 1.0, 0.0).astype(F32)
    has_hi = jnp.where(lax.axis_index("gx") < 3, 1.0, 0.0).astype(F32)
    for out, first in ((yup, 6), (ydn, 0)):
        for piece in range(5):
            if piece < 4:
                src, base = (u, 0) if piece < 2 else (kap, 16)
                y = first + piece % 2
                out[16 * piece : 16 * piece + 1] = has_lo * xlo[base + 8 + y : base + 9 + y]
                out[16 * piece + 9 : 16 * piece + 10] = has_hi * xhi[base + y : base + y + 1]
            else:
                src = g0
                y = 7 if first else 0
            for x in range(8):
                at_row = 16 * piece + 1 + x
                out[at_row : at_row + 1] = src[8 * x + y : 8 * x + y + 1]


def fine_kernel(omega, u, kap, g0, q1s, xlo, xhi, ylo, yhi, both, up, kp, gp, u1):
    gx, gy = lax.axis_index("gx"), lax.axis_index("gy")
    zero = jnp.zeros((24, 256), F32)
    for ref in (up, kp, gp):
        for x in range(12):
            ref[x] = zero
    for x in range(8):
        rows = slice(8 * x, 8 * x + 8)
        up[2 + x, 8:16] = u[rows]
        kp[2 + x, 8:16] = kap[rows]
        gp[2 + x, 8:16] = g0[rows]

    @pl.when(gx > 0)
    def _():
        for i in range(2):
            up[i, 8:16] = xlo[8 * i : 8 * i + 8]
            kp[i, 8:16] = xlo[16 + 8 * i : 24 + 8 * i]
        gp[1, 8:16] = xlo[32:40]

    @pl.when(gx < 3)
    def _():
        for i in range(2):
            up[10 + i, 8:16] = xhi[8 * i : 8 * i + 8]
            kp[10 + i, 8:16] = xhi[16 + 8 * i : 24 + 8 * i]
        gp[10, 8:16] = xhi[32:40]

    for cond, ref, row in ((gy > 0, ylo, 6), (gy < 3, yhi, 16)):

        @pl.when(cond)
        def _(ref=ref, row=row):
            for x in range(10):
                for i in range(2):
                    up[1 + x, row + i : row + i + 1] = ref[16 * i + x : 16 * i + x + 1]
                    kp[1 + x, row + i : row + i + 1] = ref[32 + 16 * i + x : 33 + 16 * i + x]
                if 1 <= x <= 8:
                    near = 7 if row == 6 else 16
                    gp[1 + x, near : near + 1] = ref[64 + x : 65 + x]

    z = lax.broadcasted_iota(jnp.int32, (24, 256), 1)

    def above(v):
        return jnp.where(z == 255, 0.0, pltpu.roll(v, 255, 1))

    def below(v):
        return jnp.where(z == 0, 0.0, pltpu.roll(v, 1, 1))

    def laplace(ref, x):
        uc, kc = ref[x], kp[x]
        total = jnp.zeros((24, 256), F32)
        for near_u, near_k in (
            (ref[x + 1], kp[x + 1]),
            (ref[x - 1], kp[x - 1]),
            (pltpu.roll(uc, 23, 0), pltpu.roll(kc, 23, 0)),
            (pltpu.roll(uc, 1, 0), pltpu.roll(kc, 1, 0)),
            (above(uc), above(kc)),
            (below(uc), below(kc)),
        ):
            total += (kc + near_k) * (near_u - uc)
        return 0.5 * total

    for x in range(1, 11):
        change = (0.5 * STEP) * (laplace(up, x) + gp[x])
        u1[x] = up[x] + change
        gp[x] = change

    @pl.when(gx == 0)
    def _():
        u1[1] = zero

    @pl.when(gx == 3)
    def _():
        u1[10] = zero

    @pl.when(gy == 0)
    def _():
        for x in range(1, 11):
            u1[x, 0:8] = zero[0:8]

    @pl.when(gy == 3)
    def _():
        for x in range(1, 11):
            u1[x, 16:24] = zero[0:8]

    first, second = [], []
    for x in range(8):
        rows = slice(8 * x, 8 * x + 8)
        c1 = gp[2 + x, 8:16]
        lap = laplace(u1, 2 + x)[8:16]
        c2 = (0.5 * STEP) * (lap + q1s[rows] - omega[0] * c1)
        first.append(c1)
        second.append(c2)
    both[:, 0:16] = jnp.concatenate(first + second, axis=0).T.reshape(16, 16, 128)
    now = jnp.concatenate([u[...], u[...]], axis=0).T.reshape(16, 16, 128)
    both[:, 16:24] = jnp.where(lane_low((16, 8, 128)), now[:, 0:8], now[:, 8:16])


def doubled(v, low):
    turned = pltpu.roll(v, 64, 1)
    return jnp.where(low, v, turned), jnp.where(low, turned, v)


def unpacked(v):
    low = lane_low((8, 128))
    first, second = doubled(v, low)
    return jnp.concatenate([first, second], axis=0)


def packed_rows(v):
    return jnp.where(lane_low((8, 128)), v[0:8], v[8:16])


def known_kernel(parts, sk, start, coef, msg, known):
    low = lane_low((16, 128))
    slab = sk[pl.ds(pl.multiple_of(lax.axis_index("tm") * 16, 16), 16), :]
    source, kap = doubled(slab, low)
    h = [start[16 * m : 16 * m + 16] for m in range(8)]
    seen = []
    for j in range(16):
        c1, c2 = doubled(parts[j, 0:16], low)
        msg[j, 136:144] = packed_rows(unpacked(parts[j, 16:24]) + c1 + c2)
        if j == 0:
            n = 2.0 * c1
            seen.append(unpacked(parts[0, 16:24]) + c1 + c2)
        else:
            q = coef[24:25] * h[0]
            for m in range(1, 8):
                q += coef[24 + m : 25 + m] * h[m]
            n = STEP * (source - (q + pltpu.roll(q, 64, 1)))
            seen.append(n + c2 - c1)
        known[j] = n
        xn = c2 - 2.0 * c1 + n
        yn = n - c1
        for m in range(8):
            h[m] = coef[m : m + 1] * h[m] + coef[16 + m : 17 + m] * (xn + coef[8 + m : 9 + m] * yn)
    last = packed_rows(kap)
    for j in range(8):
        v = jnp.where(low, seen[j], seen[j + 8])
        for p in range(16):
            msg[p, 16 * j : 16 * j + 16] = v
    for p in range(16):
        msg[p, 128:136] = last


def gather_kernel(got, own, kap, fine, up, dn):
    low = lane_low((8, 128))

    def pair(row):
        even = got[pl.ds(row, 8, stride=288), :]
        odd = got[pl.ds(row + 144, 8, stride=288), :]
        left = jnp.where(low, even, pltpu.roll(odd, 64, 1))
        right = jnp.where(low, pltpu.roll(even, 64, 1), odd)
        return left, right

    def place(j, z, v):
        own[j, z] = v
        if j < HALO:
            if z < TRI[j]:
                dn[OFF[j] + z] = v
            if z >= 16 - TRI[j]:
                up[OFF[j] + z - (16 - TRI[j])] = v

    for j in range(8):
        for z in range(16):
            left, right = pair(16 * j + z)
            place(j, z, left)
            place(j + 8, z, right)
    for z in range(8):
        fine[z], fine[z + 8] = pair(136 + z)
        left, right = pair(128 + z)
        for at, v in ((z, left), (z + 8, right)):
            kap[at] = v
            if at < HALO:
                dn[KOFF + at] = v
            if at >= 1:
                up[KOFF + at - 1] = v


def sweep_kernel(beta, own, kown, fown, lo, hi, parts_in, known_in, start_in, coef_in, out,
                 e, g, c, kw, parts, known, start, coef, sems):
    pairs = ((parts_in, parts), (known_in, known), (start_in, start), (coef_in, coef))
    copies = [pltpu.make_async_copy(a, b, sems.at[i]) for i, (a, b) in enumerate(pairs)]
    for copy in copies:
        copy.start()
    t = lax.axis_index("tm")
    has_lo = jnp.where(t > 0, 1.0, 0.0).astype(F32)
    has_hi = jnp.where(t < 15, 1.0, 0.0).astype(F32)

    def pick(j, first, last):
        if last <= HALO:
            start = OFF[j] + first - HALO + TRI[j]
            return has_lo * lo[start : start + last - first]
        if first > 30:
            start = OFF[j] + first - 31
            return has_hi * hi[start : start + last - first]
        return own[j, first - HALO : last - HALO]

    def groups(first, last):
        ranges = []
        for a, b in ((first, HALO), (HALO, 31), (31, last)):
            pieces = -(-(b - a) // GROUP)
            edge = [a + (b - a) * k // pieces for k in range(pieces + 1)] if pieces else []
            ranges += list(zip(edge[:-1], edge[1:]))
        return ranges

    zero = jnp.zeros((8, 128), F32)
    kw[0] = zero
    kw[47] = zero
    kw[1:16] = has_lo * lo[KOFF:MSG]
    kw[16:32] = kown[...]
    kw[32:47] = has_hi * hi[KOFF:MSG]

    lane = lax.broadcasted_iota(jnp.int32, (8, 128), 1)
    sub = lax.broadcasted_iota(jnp.int32, (8, 128), 0)
    x_start, x_end = lane < 8, lane >= 120
    y_start, y_end = lane % 8 == 0, lane % 8 == 7
    inside = (
        jnp.logical_not(x_end & (sub % 2 == 1)),
        jnp.logical_not(x_start & (sub % 2 == 0)),
        jnp.logical_not(y_end & (sub // 2 == 3)),
        jnp.logical_not(y_start & (sub // 2 == 0)),
    )

    def near(a):
        down, up = pltpu.roll(a, 8, 2), pltpu.roll(a, 120, 2)
        xm = jnp.where(x_start, pltpu.roll(down, 1, 1), down)
        xp = jnp.where(x_end, pltpu.roll(up, 7, 1), up)
        yp = pltpu.roll(jnp.where(y_start, pltpu.roll(down, 6, 1), a), 127, 2)
        ym = pltpu.roll(jnp.where(y_end, pltpu.roll(up, 2, 1), a), 1, 2)
        return xp, xm, yp, ym

    for first, last in groups(1, NEW - 1):
        kc = kw[first + 1 : last + 1]
        layer = lax.broadcasted_iota(jnp.int32, kc.shape, 0) + first
        place = t * 16 - HALO + layer
        scale = jnp.where((place >= 0) & (place < 256), 0.5 * STEP, 0.0).astype(F32)
        total = jnp.zeros_like(kc)
        for i, kn in enumerate(near(kc)):
            face = scale * (kc + jnp.where(inside[i], kn, 0.0))
            total += face
            c[i, first:last] = jnp.where(inside[i], face, 0.0)
        for i, kn in ((4, kw[first + 2 : last + 2]), (5, kw[first:last])):
            face = scale * (kc + kn)
            total += face
            c[i, first:last] = face
        c[6, first:last] = -total

    for first, last in groups(0, NEW):
        e[0, first:last] = pick(0, first, last)
    for j in range(1, 16):
        for first, last in groups(j, NEW - j):
            mid = e[j - 1, first:last]
            acc = c[6, first:last] * mid
            acc += c[4, first:last] * e[j - 1, first + 1 : last + 1]
            acc += c[5, first:last] * e[j - 1, first - 1 : last - 1]
            for d, un in enumerate(near(mid)):
                acc += c[d, first:last] * un
            for i in range(1, j):
                acc -= beta[j - 1 - i] * g[i, first:last]
            now = mid + acc + pick(j, first, last)
            g[j, first:last] = acc
            e[j, first:last] = now
    for copy in copies:
        copy.wait()
    low = lane_low((16, 128))
    p = lax.axis_index("gy") * 4 + lax.axis_index("gx")
    sublane = p // 2
    mine = low == (p % 2 == 0)
    e_rows = e.reshape(16 * LAY * 8, 128)
    g_rows = g.reshape(16 * LAY * 8, 128)

    def block_of(ref, j):
        first = (j * LAY + HALO) * 8 + sublane
        a = ref[pl.ds(first, 8, stride=8), :]
        b = ref[pl.ds(first + 64, 8, stride=8), :]
        both = jnp.concatenate([a, b], axis=0)
        return jnp.where(mine, both, pltpu.roll(both, 64, 1))

    h = [start[16 * m : 16 * m + 16] for m in range(8)]
    for j in range(16):
        c1, c2 = doubled(parts[j, 0:16], low)
        n = known[j]
        if j > 0:
            n = n + block_of(g_rows, j)
        xn = c2 - 2.0 * c1 + n
        yn = n - c1
        for m in range(8):
            h[m] = coef[m : m + 1] * h[m] + coef[16 + m : 17 + m] * (xn + coef[8 + m : 9 + m] * yn)
            if j % 2 == 0:
                at_row = 16 * (m % 4)
                out[j + m // 4, at_row : at_row + 16] = h[m]
        out[j, 64:72] = packed_rows(block_of(e_rows, j))
    diff = e[p, HALO:31] - fown[...]
    part = jnp.sum(diff * diff, axis=0)
    for j in range(16):
        out[j, 72:80] = part


def rows_of(ref):
    return jnp.concatenate([unpacked(ref[t, 64:72]) for t in range(16)], axis=0)


def size_kernel(got, size):
    part = got[0, 72:80]
    for t in range(1, 16):
        part += got[t, 72:80]
    whole = jnp.sum(jnp.sum(part, axis=1, keepdims=True), axis=0, keepdims=True)
    size[0] = jnp.sqrt(whole / 262144.0)[0, 0]


def field_kernel(got, field):
    field[...] = rows_of(got).T[0:64]


def final_kernel(got, other, mine, coef, modes):
    def finish(low, high, odd):
        x = y = None
        if odd:
            c1, c2 = doubled(mine[:, 0:16].reshape(256, 128), lane_low((256, 128)))
            x = rows_of(high) - rows_of(low) - c1
            y = x - c2 + c1
        for m in range(8):
            src = low if m < 4 else high
            first = 16 * (m % 4)
            both = src[:, first : first + 16].reshape(256, 128)
            if odd:
                both = coef[m : m + 1] * both
                both += coef[16 + m : 17 + m] * (x + coef[8 + m : 9 + m] * y)
            both = both.T
            modes[m] = both[0:64]
            modes[m + 8] = both[64:128]

    t = lax.axis_index("tm")

    @pl.when(t % 2 == 0)
    def _():
        finish(got, other, False)

    @pl.when(t % 2 == 1)
    def _():
        finish(other, got, True)


def ring(axis, step):
    n = lax.axis_size(axis)
    return [(i, (i + step) % n) for i in range(n)]


def turned():
    def apart(a, b, n):
        return min((a - b) % n, (b - a) % n)

    def device(t, p):
        return 16 * t + p % 4 * 4 + p // 4

    pairs = []
    for j in range(16):
        far = sorted(range(16), key=lambda p: -apart(p % 4, j % 4, 4) - apart(p // 4, j // 4, 4))
        near = sorted(range(16), key=lambda t: apart(t // 2, j // 2, 8))
        pairs += [(device(t, j), device(j, p)) for t, p in zip(near, far)]
    return pairs


def swap(value, axis):
    return lax.all_to_all(value, axis, 0, 0, tiled=True)


def per_device(field, modes, source, regions, region_kappa, mode_rate, mode_weight):
    u = field.reshape(64, 256)
    h = modes.reshape(16, 64, 256)
    s = source.reshape(64, 256)
    reg = regions.reshape(64, 256)
    t = lax.axis_index("tm")

    f = jnp.exp(-0.5 * mode_rate)
    e = jnp.exp(-mode_rate)
    w = mode_weight
    omega = jnp.sum(w * (1.0 - f)).reshape(1)
    powers = jnp.exp(-mode_rate[None, :] * jnp.arange(16, dtype=F32)[:, None])
    beta = STEP * jnp.sum((w * (1.0 - e))[None, :] * powers, axis=1)
    coef = jnp.concatenate([e, f, 1.0 - f, w]).reshape(4, 2, 8).transpose(0, 2, 1)
    coef = jnp.broadcast_to(coef[..., None], (4, 8, 2, 64)).reshape(32, 128)

    plane = (64, 256)
    outs = [plane] * 4 + [(40, 256)] * 2 + [(256, 128)]
    u, kap, g0, q1s, up, dn, sk = pl.pallas_call(
        local_kernel,
        out_shape=[jax.ShapeDtypeStruct(shape, F32) for shape in outs],
        in_specs=[ANY] * 7,
        out_specs=[VM] * 7,
        scratch_shapes=[pltpu.SMEM((8,), F32), pltpu.SMEM((16,), F32), pltpu.SMEM((16,), F32)]
        + [pltpu.VMEM(plane, jnp.int32), pltpu.VMEM(plane, F32), pltpu.VMEM((16, 64, 256), F32)]
        + [pltpu.SemaphoreType.DMA((10,))],
        compiler_params=pltpu.CompilerParams(vmem_limit_bytes=60 * MIB),
    )(region_kappa, w, mode_rate, u, reg, s, h)
    xlo = lax.ppermute(up, "gx", ring("gx", 1))
    xhi = lax.ppermute(dn, "gx", ring("gx", -1))
    chunks = pl.pallas_call(
        scatter_kernel,
        out_shape=[jax.ShapeDtypeStruct((4, 128, 128), F32)] * 4,
        in_specs=[ANY, ANY],
        out_specs=[ANY] * 4,
        scratch_shapes=[pltpu.VMEM((16, 64, 256), F32), pltpu.VMEM((16, 128, 128), F32)]
        + [pltpu.SemaphoreType.DMA((8,))],
        compiler_params=pltpu.CompilerParams(vmem_limit_bytes=60 * MIB),
    )(sk, h)

    yup, ydn = call(side_kernel, [(80, 256)] * 2, 5, 0)(u, kap, g0, xlo, xhi)
    ylo = lax.ppermute(yup, "gy", ring("gy", 1))
    yhi = lax.ppermute(ydn, "gy", ring("gy", -1))
    far = [lax.ppermute(chunks[k], "tm", [(0, 4 * k)]) for k in (2, 3, 1)]

    (both,) = call(
        fine_kernel, [(16, 24, 128)], 9, 1, [(12, 24, 256)] * 4, 16, LONG
    )(omega, u, kap, g0, q1s, xlo, xhi, ylo, yhi)
    parts = swap(both, "tm")

    share = jnp.where(t == 0, chunks[0], far[0] + far[1] + far[2])
    close = [
        lax.ppermute(share[k], "tm", [(4 * a, 4 * a + k) for a in range(4)]) for k in (1, 2, 3)
    ]
    start = jnp.where(t % 4 == 0, share[0], close[0] + close[1] + close[2])

    msg, known = call(known_kernel, [(16, 144, 128), (16, 16, 128)], 4, 0)(
        parts, sk, start, coef
    )
    got = swap(msg, ("gy", "gx"))
    own, kown, fown, up, dn = call(
        gather_kernel,
        [(16, 16, 8, 128), (16, 8, 128), (16, 8, 128), (MSG, 8, 128), (MSG, 8, 128)],
        1,
        0,
    )(got.reshape(16 * 144, 128))
    lo = lax.ppermute(up, "tm", ring("tm", 1))
    hi = lax.ppermute(dn, "tm", ring("tm", -1))
    out = pl.pallas_call(
        sweep_kernel,
        out_shape=jax.ShapeDtypeStruct((16, 80, 128), F32),
        in_specs=[SM] + [VM] * 5 + [ANY] * 4,
        out_specs=VM,
        scratch_shapes=[
            pltpu.VMEM(shape, F32)
            for shape in (
                (16, LAY, 8, 128),
                (16, LAY, 8, 128),
                (7, LAY, 8, 128),
                (LAY, 8, 128),
                (16, 24, 128),
                (16, 16, 128),
                (128, 128),
                (32, 128),
            )
        ]
        + [pltpu.SemaphoreType.DMA((4,))],
        compiler_params=pltpu.CompilerParams(vmem_limit_bytes=24 * MIB),
    )(beta, own, kown, fown, lo, hi, parts, known, start, coef)
    back = swap(out, "tm")
    other = lax.ppermute(back, "tm", [(i, i ^ 1) for i in range(16)])
    size = pl.pallas_call(
        size_kernel,
        out_shape=jax.ShapeDtypeStruct((1,), F32),
        in_specs=[VM],
        out_specs=SM,
        compiler_params=pltpu.CompilerParams(vmem_limit_bytes=16 * MIB),
    )(back)
    size = lax.ppermute(size, ("tm", "gx", "gy"), turned())
    new_field = call(field_kernel, [plane], 1, 0)(back)[0]
    new_modes = call(final_kernel, [(16, 64, 256)], 4, 0)(back, other, both, coef)[0]
    size, new_modes, new_field = lax.optimization_barrier((size, new_modes, new_field))
    return (new_field.reshape(1, 8, 8, 256), new_modes.reshape(1, 16, 8, 8, 256), size)


def solution(mesh):
    return jax.shard_map(
        per_device,
        mesh=mesh,
        in_specs=(
            P("tm", "gx", "gy", None),
            P("tm", None, "gx", "gy", None),
            P("gx", "gy", None),
            P("gx", "gy", None),
            P(),
            P(),
            P(),
        ),
        out_specs=(P("tm", "gx", "gy", None), P("tm", None, "gx", "gy", None), P("tm")),
        check_vma=False,
    )
```

```python
import functools
import jax
import jax.numpy as jnp
from jax import lax
from jax.experimental import pallas as pl
from jax.experimental.pallas import tpu as pltpu
from jax.sharding import PartitionSpec as P

STEP = 0.12
F32 = jnp.float32
VM = pl.BlockSpec(memory_space=pltpu.VMEM)
SM = pl.BlockSpec(memory_space=pltpu.SMEM)
ANY = pl.BlockSpec(memory_space=pl.ANY)
MIB = 1024 * 1024
LONG = pl.CostEstimate(flops=20_000_000_000, bytes_accessed=1_000_000, transcendentals=0)
SLOTS = [0, 2, 3, 10, 9, 1, 4, 5, 6, 7, 8, 0, 12, 13, 14, 15, 11, 0]
HALO = 15
TRI = [HALO] + [HALO - j for j in range(1, HALO)]
OFF = [sum(TRI[:j]) for j in range(HALO)]
KOFF = sum(TRI)
MSG = KOFF + HALO
LAY = 48
NEW = 46
GROUP = 16


def call(kernel, outs, ins, smem, scratch=(), limit=16, cost=None):
    return pl.pallas_call(
        kernel,
        out_shape=[jax.ShapeDtypeStruct(shape, F32) for shape in outs],
        in_specs=[SM] * smem + [VM] * (ins - smem),
        out_specs=[VM] * len(outs),
        scratch_shapes=[pltpu.VMEM(shape, F32) for shape in scratch],
        compiler_params=pltpu.CompilerParams(vmem_limit_bytes=limit * MIB),
        cost_estimate=cost,
    )


def lane_low(shape):
    return lax.broadcasted_iota(jnp.int32, shape, len(shape) - 1) < 64


def local_kernel(rk_in, w_in, rate_in, u_in, reg_in, s_in, modes_in, u, kap, g0, q1s, up, dn, sk,
                 rk, w, rate, reg, s, modes, sems):
    pairs = [(u_in, u), (reg_in, reg), (s_in, s), (rk_in, rk), (w_in, w), (rate_in, rate)]
    pairs += [(modes_in.at[pl.ds(4 * i, 4)], modes.at[pl.ds(4 * i, 4)]) for i in range(4)]
    copies = [pltpu.make_async_copy(a, b, sems.at[i]) for i, (a, b) in enumerate(pairs)]
    for copy in copies:
        copy.start()
    for copy in copies[:6]:
        copy.wait()
    for x in range(8):
        rows = slice(8 * x, 8 * x + 8)
        region = reg[rows]
        k = jnp.zeros((8, 256), F32)
        for r in range(8):
            k = jnp.where(region == r, rk[r], k)
        kap[rows] = k
    half = [jnp.exp(jnp.full((8, 256), -0.5 * rate[m], F32)) for m in range(16)]
    a = [s[8 * x : 8 * x + 8] for x in range(8)]
    b = [s[8 * x : 8 * x + 8] for x in range(8)]
    for m in range(16):
        if m % 4 == 0:
            copies[6 + m // 4].wait()
        for x in range(8):
            h = w[m] * modes[m, 8 * x : 8 * x + 8]
            a[x] = a[x] - h
            b[x] = b[x] - half[m] * h
    for x in range(8):
        g0[8 * x : 8 * x + 8] = a[x]
        q1s[8 * x : 8 * x + 8] = b[x]
    up[0:16] = u[48:64]
    up[16:32] = kap[48:64]
    up[32:40] = g0[56:64]
    dn[0:16] = u[0:16]
    dn[16:32] = kap[0:16]
    dn[32:40] = g0[0:8]
    sk[...] = jnp.concatenate([s[...], kap[...]], axis=0).T


def scatter_kernel(after, modes_in, out0, out1, out2, modes, packed, sems):
    @pl.when(lax.axis_index("tm") == 0)
    def _():
        copies = [
            pltpu.make_async_copy(modes_in.at[pl.ds(4 * i, 4)], modes.at[pl.ds(4 * i, 4)], sems.at[i])
            for i in range(4)
        ]
        for copy in copies:
            copy.start()
        for copy in copies:
            copy.wait()
        for m in range(8):
            both = jnp.concatenate([modes[m], modes[m + 8]], axis=0).T
            pieces = both.reshape(16, 16, 128)
            for place, slot in enumerate(SLOTS):
                packed[place, 16 * m : 16 * m + 16] = pieces[slot]
        copies = [
            pltpu.make_async_copy(packed.at[pl.ds(6 * i, 6)], out, sems.at[4 + i])
            for i, out in enumerate((out0, out1, out2))
        ]
        for copy in copies:
            copy.start()
        for copy in copies:
            copy.wait()


def side_kernel(u, kap, g0, xlo, xhi, yup, ydn):
    has_lo = jnp.where(lax.axis_index("gx") > 0, 1.0, 0.0).astype(F32)
    has_hi = jnp.where(lax.axis_index("gx") < 3, 1.0, 0.0).astype(F32)
    for out, first in ((yup, 6), (ydn, 0)):
        for piece in range(5):
            if piece < 4:
                src, base = (u, 0) if piece < 2 else (kap, 16)
                y = first + piece % 2
                out[16 * piece : 16 * piece + 1] = has_lo * xlo[base + 8 + y : base + 9 + y]
                out[16 * piece + 9 : 16 * piece + 10] = has_hi * xhi[base + y : base + y + 1]
            else:
                src = g0
                y = 7 if first else 0
            for x in range(8):
                at_row = 16 * piece + 1 + x
                out[at_row : at_row + 1] = src[8 * x + y : 8 * x + y + 1]


def fine_kernel(omega, u, kap, g0, q1s, xlo, xhi, ylo, yhi, both, up, kp, gp, u1):
    gx, gy = lax.axis_index("gx"), lax.axis_index("gy")
    zero = jnp.zeros((24, 256), F32)
    for ref in (up, kp, gp):
        for x in range(12):
            ref[x] = zero
    for x in range(8):
        rows = slice(8 * x, 8 * x + 8)
        up[2 + x, 8:16] = u[rows]
        kp[2 + x, 8:16] = kap[rows]
        gp[2 + x, 8:16] = g0[rows]

    @pl.when(gx > 0)
    def _():
        for i in range(2):
            up[i, 8:16] = xlo[8 * i : 8 * i + 8]
            kp[i, 8:16] = xlo[16 + 8 * i : 24 + 8 * i]
        gp[1, 8:16] = xlo[32:40]

    @pl.when(gx < 3)
    def _():
        for i in range(2):
            up[10 + i, 8:16] = xhi[8 * i : 8 * i + 8]
            kp[10 + i, 8:16] = xhi[16 + 8 * i : 24 + 8 * i]
        gp[10, 8:16] = xhi[32:40]

    for cond, ref, row in ((gy > 0, ylo, 6), (gy < 3, yhi, 16)):

        @pl.when(cond)
        def _(ref=ref, row=row):
            for x in range(10):
                for i in range(2):
                    up[1 + x, row + i : row + i + 1] = ref[16 * i + x : 16 * i + x + 1]
                    kp[1 + x, row + i : row + i + 1] = ref[32 + 16 * i + x : 33 + 16 * i + x]
                if 1 <= x <= 8:
                    near = 7 if row == 6 else 16
                    gp[1 + x, near : near + 1] = ref[64 + x : 65 + x]

    z = lax.broadcasted_iota(jnp.int32, (24, 256), 1)

    def above(v):
        return jnp.where(z == 255, 0.0, pltpu.roll(v, 255, 1))

    def below(v):
        return jnp.where(z == 0, 0.0, pltpu.roll(v, 1, 1))

    def laplace(ref, x):
        uc, kc = ref[x], kp[x]
        total = jnp.zeros((24, 256), F32)
        for near_u, near_k in (
            (ref[x + 1], kp[x + 1]),
            (ref[x - 1], kp[x - 1]),
            (pltpu.roll(uc, 23, 0), pltpu.roll(kc, 23, 0)),
            (pltpu.roll(uc, 1, 0), pltpu.roll(kc, 1, 0)),
            (above(uc), above(kc)),
            (below(uc), below(kc)),
        ):
            total += (kc + near_k) * (near_u - uc)
        return 0.5 * total

    for x in range(1, 11):
        change = (0.5 * STEP) * (laplace(up, x) + gp[x])
        u1[x] = up[x] + change
        gp[x] = change

    @pl.when(gx == 0)
    def _():
        u1[1] = zero

    @pl.when(gx == 3)
    def _():
        u1[10] = zero

    @pl.when(gy == 0)
    def _():
        for x in range(1, 11):
            u1[x, 0:8] = zero[0:8]

    @pl.when(gy == 3)
    def _():
        for x in range(1, 11):
            u1[x, 16:24] = zero[0:8]

    first, second = [], []
    for x in range(8):
        rows = slice(8 * x, 8 * x + 8)
        c1 = gp[2 + x, 8:16]
        lap = laplace(u1, 2 + x)[8:16]
        c2 = (0.5 * STEP) * (lap + q1s[rows] - omega[0] * c1)
        first.append(c1)
        second.append(c2)
    both[:, 0:16] = jnp.concatenate(first + second, axis=0).T.reshape(16, 16, 128)
    now = jnp.concatenate([u[...], u[...]], axis=0).T.reshape(16, 16, 128)
    both[:, 16:24] = jnp.where(lane_low((16, 8, 128)), now[:, 0:8], now[:, 8:16])


def doubled(v, low):
    turned = pltpu.roll(v, 64, 1)
    return jnp.where(low, v, turned), jnp.where(low, turned, v)


def unpacked(v):
    low = lane_low((8, 128))
    first, second = doubled(v, low)
    return jnp.concatenate([first, second], axis=0)


def packed_rows(v):
    return jnp.where(lane_low((8, 128)), v[0:8], v[8:16])


def known_kernel(parts, sk, start, coef, msg, known):
    low = lane_low((16, 128))
    slab = sk[pl.ds(pl.multiple_of(lax.axis_index("tm") * 16, 16), 16), :]
    source, kap = doubled(slab, low)
    h = [start[16 * m : 16 * m + 16] for m in range(8)]
    seen = []
    for j in range(16):
        c1, c2 = doubled(parts[j, 0:16], low)
        msg[j, 136:144] = packed_rows(unpacked(parts[j, 16:24]) + c1 + c2)
        if j == 0:
            n = 2.0 * c1
            seen.append(unpacked(parts[0, 16:24]) + c1 + c2)
        else:
            q = coef[24:25] * h[0]
            for m in range(1, 8):
                q += coef[24 + m : 25 + m] * h[m]
            n = STEP * (source - (q + pltpu.roll(q, 64, 1)))
            seen.append(n + c2 - c1)
        known[j] = n
        xn = c2 - 2.0 * c1 + n
        yn = n - c1
        for m in range(8):
            h[m] = coef[m : m + 1] * h[m] + coef[16 + m : 17 + m] * (xn + coef[8 + m : 9 + m] * yn)
    last = packed_rows(kap)
    for j in range(8):
        v = jnp.where(low, seen[j], seen[j + 8])
        for p in range(16):
            msg[p, 16 * j : 16 * j + 16] = v
    for p in range(16):
        msg[p, 128:136] = last


def gather_kernel(got, own, kap, fine, up, dn):
    low = lane_low((8, 128))

    def pair(row):
        even = got[pl.ds(row, 8, stride=288), :]
        odd = got[pl.ds(row + 144, 8, stride=288), :]
        left = jnp.where(low, even, pltpu.roll(odd, 64, 1))
        right = jnp.where(low, pltpu.roll(even, 64, 1), odd)
        return left, right

    def place(j, z, v):
        own[j, z] = v
        if j < HALO:
            if z < TRI[j]:
                dn[OFF[j] + z] = v
            if z >= 16 - TRI[j]:
                up[OFF[j] + z - (16 - TRI[j])] = v

    for j in range(8):
        for z in range(16):
            left, right = pair(16 * j + z)
            place(j, z, left)
            place(j + 8, z, right)
    for z in range(8):
        fine[z], fine[z + 8] = pair(136 + z)
        left, right = pair(128 + z)
        for at, v in ((z, left), (z + 8, right)):
            kap[at] = v
            if at < HALO:
                dn[KOFF + at] = v
            if at >= 1:
                up[KOFF + at - 1] = v


def sweep_kernel(beta, own, kown, fown, lo, hi, parts_in, known_in, start_in, coef_in, out,
                 e, g, c, kw, parts, known, start, coef, sems):
    pairs = ((parts_in, parts), (known_in, known), (start_in, start), (coef_in, coef))
    copies = [pltpu.make_async_copy(a, b, sems.at[i]) for i, (a, b) in enumerate(pairs)]
    for copy in copies:
        copy.start()
    t = lax.axis_index("tm")
    has_lo = jnp.where(t > 0, 1.0, 0.0).astype(F32)
    has_hi = jnp.where(t < 15, 1.0, 0.0).astype(F32)

    def pick(j, first, last):
        if last <= HALO:
            start = OFF[j] + first - HALO + TRI[j]
            return has_lo * lo[start : start + last - first]
        if first > 30:
            start = OFF[j] + first - 31
            return has_hi * hi[start : start + last - first]
        return own[j, first - HALO : last - HALO]

    def groups(first, last):
        ranges = []
        for a, b in ((first, HALO), (HALO, 31), (31, last)):
            pieces = -(-(b - a) // GROUP)
            edge = [a + (b - a) * k // pieces for k in range(pieces + 1)] if pieces else []
            ranges += list(zip(edge[:-1], edge[1:]))
        return ranges

    zero = jnp.zeros((8, 128), F32)
    kw[0] = zero
    kw[47] = zero
    kw[1:16] = has_lo * lo[KOFF:MSG]
    kw[16:32] = kown[...]
    kw[32:47] = has_hi * hi[KOFF:MSG]

    lane = lax.broadcasted_iota(jnp.int32, (8, 128), 1)
    sub = lax.broadcasted_iota(jnp.int32, (8, 128), 0)
    x_start, x_end = lane < 8, lane >= 120
    y_start, y_end = lane % 8 == 0, lane % 8 == 7
    inside = (
        jnp.logical_not(x_end & (sub % 2 == 1)),
        jnp.logical_not(x_start & (sub % 2 == 0)),
        jnp.logical_not(y_end & (sub // 2 == 3)),
        jnp.logical_not(y_start & (sub // 2 == 0)),
    )

    def near(a):
        down, up = pltpu.roll(a, 8, 2), pltpu.roll(a, 120, 2)
        xm = jnp.where(x_start, pltpu.roll(down, 1, 1), down)
        xp = jnp.where(x_end, pltpu.roll(up, 7, 1), up)
        yp = pltpu.roll(jnp.where(y_start, pltpu.roll(down, 6, 1), a), 127, 2)
        ym = pltpu.roll(jnp.where(y_end, pltpu.roll(up, 2, 1), a), 1, 2)
        return xp, xm, yp, ym

    for first, last in groups(1, NEW - 1):
        kc = kw[first + 1 : last + 1]
        layer = lax.broadcasted_iota(jnp.int32, kc.shape, 0) + first
        place = t * 16 - HALO + layer
        scale = jnp.where((place >= 0) & (place < 256), 0.5 * STEP, 0.0).astype(F32)
        total = jnp.zeros_like(kc)
        for i, kn in enumerate(near(kc)):
            face = scale * (kc + jnp.where(inside[i], kn, 0.0))
            total += face
            c[i, first:last] = jnp.where(inside[i], face, 0.0)
        for i, kn in ((4, kw[first + 2 : last + 2]), (5, kw[first:last])):
            face = scale * (kc + kn)
            total += face
            c[i, first:last] = face
        c[6, first:last] = -total

    for first, last in groups(0, NEW):
        e[0, first:last] = pick(0, first, last)
    for j in range(1, 16):
        for first, last in groups(j, NEW - j):
            mid = e[j - 1, first:last]
            acc = c[6, first:last] * mid
            acc += c[4, first:last] * e[j - 1, first + 1 : last + 1]
            acc += c[5, first:last] * e[j - 1, first - 1 : last - 1]
            for d, un in enumerate(near(mid)):
                acc += c[d, first:last] * un
            for i in range(1, j):
                acc -= beta[j - 1 - i] * g[i, first:last]
            now = mid + acc + pick(j, first, last)
            g[j, first:last] = acc
            e[j, first:last] = now
    for copy in copies:
        copy.wait()
    low = lane_low((16, 128))
    p = lax.axis_index("gy") * 4 + lax.axis_index("gx")
    sublane = p // 2
    mine = low == (p % 2 == 0)
    e_rows = e.reshape(16 * LAY * 8, 128)
    g_rows = g.reshape(16 * LAY * 8, 128)

    def block_of(ref, j):
        first = (j * LAY + HALO) * 8 + sublane
        a = ref[pl.ds(first, 8, stride=8), :]
        b = ref[pl.ds(first + 64, 8, stride=8), :]
        both = jnp.concatenate([a, b], axis=0)
        return jnp.where(mine, both, pltpu.roll(both, 64, 1))

    h = [start[16 * m : 16 * m + 16] for m in range(8)]
    for j in range(16):
        c1, c2 = doubled(parts[j, 0:16], low)
        n = known[j]
        if j > 0:
            n = n + block_of(g_rows, j)
        xn = c2 - 2.0 * c1 + n
        yn = n - c1
        for m in range(8):
            h[m] = coef[m : m + 1] * h[m] + coef[16 + m : 17 + m] * (xn + coef[8 + m : 9 + m] * yn)
            if j % 2 == 0:
                at_row = 16 * (m % 4)
                out[j + m // 4, at_row : at_row + 16] = h[m]
        out[j, 64:72] = packed_rows(block_of(e_rows, j))
    diff = e[p, HALO:31] - fown[...]
    part = jnp.sum(diff * diff, axis=0)
    for j in range(16):
        out[j, 72:80] = part


def rows_of(ref):
    return jnp.concatenate([unpacked(ref[t, 64:72]) for t in range(16)], axis=0)


def field_kernel(got, field, size):
    field[...] = rows_of(got).T[0:64]
    part = got[0, 72:80]
    for t in range(1, 16):
        part += got[t, 72:80]
    whole = jnp.sum(jnp.sum(part, axis=1, keepdims=True), axis=0, keepdims=True)
    size[0] = jnp.sqrt(whole / 262144.0)[0, 0]


def final_kernel(got, other, mine, coef, modes):
    def finish(low, high, odd):
        x = y = None
        if odd:
            c1, c2 = doubled(mine[:, 0:16].reshape(256, 128), lane_low((256, 128)))
            x = rows_of(high) - rows_of(low) - c1
            y = x - c2 + c1
        for m in range(8):
            src = low if m < 4 else high
            first = 16 * (m % 4)
            both = src[:, first : first + 16].reshape(256, 128)
            if odd:
                both = coef[m : m + 1] * both
                both += coef[16 + m : 17 + m] * (x + coef[8 + m : 9 + m] * y)
            both = both.T
            modes[m] = both[0:64]
            modes[m + 8] = both[64:128]

    t = lax.axis_index("tm")

    @pl.when(t % 2 == 0)
    def _():
        finish(got, other, False)

    @pl.when(t % 2 == 1)
    def _():
        finish(other, got, True)


def ring(axis, step):
    n = lax.axis_size(axis)
    return [(i, (i + step) % n) for i in range(n)]


def turned():
    def apart(a, b, n):
        return min((a - b) % n, (b - a) % n)

    def device(t, p):
        return 16 * t + p % 4 * 4 + p // 4

    pairs = []
    for j in range(16):
        far = sorted(range(16), key=lambda p: -apart(p % 4, j % 4, 4) - apart(p // 4, j // 4, 4))
        near = sorted(range(16), key=lambda t: apart(t // 2, j // 2, 8))
        pairs += [(device(t, j), device(j, p)) for t, p in zip(near, far)]
    return pairs


def swap(value, axis):
    return lax.all_to_all(value, axis, 0, 0, tiled=True)


def per_device(field, modes, source, regions, region_kappa, mode_rate, mode_weight):
    u = field.reshape(64, 256)
    h = modes.reshape(16, 64, 256)
    s = source.reshape(64, 256)
    reg = regions.reshape(64, 256)
    t = lax.axis_index("tm")

    f = jnp.exp(-0.5 * mode_rate)
    e = jnp.exp(-mode_rate)
    w = mode_weight
    omega = jnp.sum(w * (1.0 - f)).reshape(1)
    powers = jnp.exp(-mode_rate[None, :] * jnp.arange(16, dtype=F32)[:, None])
    beta = STEP * jnp.sum((w * (1.0 - e))[None, :] * powers, axis=1)
    coef = jnp.concatenate([e, f, 1.0 - f, w]).reshape(4, 2, 8).transpose(0, 2, 1)
    coef = jnp.broadcast_to(coef[..., None], (4, 8, 2, 64)).reshape(32, 128)

    plane = (64, 256)
    outs = [plane] * 4 + [(40, 256)] * 2 + [(256, 128)]
    u, kap, g0, q1s, up, dn, sk = pl.pallas_call(
        local_kernel,
        out_shape=[jax.ShapeDtypeStruct(shape, F32) for shape in outs],
        in_specs=[ANY] * 7,
        out_specs=[VM] * 7,
        scratch_shapes=[pltpu.SMEM((8,), F32), pltpu.SMEM((16,), F32), pltpu.SMEM((16,), F32)]
        + [pltpu.VMEM(plane, jnp.int32), pltpu.VMEM(plane, F32), pltpu.VMEM((16, 64, 256), F32)]
        + [pltpu.SemaphoreType.DMA((10,))],
        compiler_params=pltpu.CompilerParams(vmem_limit_bytes=60 * MIB),
    )(region_kappa, w, mode_rate, u, reg, s, h)
    xlo = lax.ppermute(up, "gx", ring("gx", 1))
    xhi = lax.ppermute(dn, "gx", ring("gx", -1))
    chunks = pl.pallas_call(
        scatter_kernel,
        out_shape=[jax.ShapeDtypeStruct((6, 128, 128), F32)] * 3,
        in_specs=[ANY, ANY],
        out_specs=[ANY] * 3,
        scratch_shapes=[pltpu.VMEM((16, 64, 256), F32), pltpu.VMEM((18, 128, 128), F32)]
        + [pltpu.SemaphoreType.DMA((7,))],
        compiler_params=pltpu.CompilerParams(vmem_limit_bytes=60 * MIB),
    )(sk, h)

    yup, ydn = call(side_kernel, [(80, 256)] * 2, 5, 0)(u, kap, g0, xlo, xhi)
    ylo = lax.ppermute(yup, "gy", ring("gy", 1))
    yhi = lax.ppermute(ydn, "gy", ring("gy", -1))
    far = [lax.ppermute(chunks[k], "tm", [(0, hub)]) for k, hub in ((1, 4), (2, 12))]

    (both,) = call(
        fine_kernel, [(16, 24, 128)], 9, 1, [(12, 24, 256)] * 4, 16, LONG
    )(omega, u, kap, g0, q1s, xlo, xhi, ylo, yhi)
    parts = swap(both, "tm")

    share = jnp.where(t == 0, chunks[0], far[0] + far[1])
    pairs = [
        [(0, 2), (4, 5), (12, 13)],
        [(0, 3), (4, 6), (12, 14)],
        [(0, 10), (4, 7), (12, 15)],
        [(0, 9), (4, 8), (12, 11)],
        [(0, 1)],
    ]
    close = [lax.ppermute(share[k + 1], "tm", pair) for k, pair in enumerate(pairs)]
    hub = (t == 0) | (t == 4) | (t == 12)
    start = jnp.where(hub, share[0], sum(close))

    msg, known = call(known_kernel, [(16, 144, 128), (16, 16, 128)], 4, 0)(
        parts, sk, start, coef
    )
    got = swap(msg, ("gy", "gx"))
    own, kown, fown, up, dn = call(
        gather_kernel,
        [(16, 16, 8, 128), (16, 8, 128), (16, 8, 128), (MSG, 8, 128), (MSG, 8, 128)],
        1,
        0,
    )(got.reshape(16 * 144, 128))
    lo = lax.ppermute(up, "tm", ring("tm", 1))
    hi = lax.ppermute(dn, "tm", ring("tm", -1))
    out = pl.pallas_call(
        sweep_kernel,
        out_shape=jax.ShapeDtypeStruct((16, 80, 128), F32),
        in_specs=[SM] + [VM] * 5 + [ANY] * 4,
        out_specs=VM,
        scratch_shapes=[
            pltpu.VMEM(shape, F32)
            for shape in (
                (16, LAY, 8, 128),
                (16, LAY, 8, 128),
                (7, LAY, 8, 128),
                (LAY, 8, 128),
                (16, 24, 128),
                (16, 16, 128),
                (128, 128),
                (32, 128),
            )
        ]
        + [pltpu.SemaphoreType.DMA((4,))],
        compiler_params=pltpu.CompilerParams(vmem_limit_bytes=24 * MIB),
    )(beta, own, kown, fown, lo, hi, parts, known, start, coef)
    back = swap(out, "tm")
    other = lax.ppermute(back, "tm", [(i, i ^ 1) for i in range(16)])
    new_field, size = pl.pallas_call(
        field_kernel,
        out_shape=[jax.ShapeDtypeStruct(shape, F32) for shape in (plane, (1,))],
        in_specs=[VM],
        out_specs=[VM, SM],
        compiler_params=pltpu.CompilerParams(vmem_limit_bytes=16 * MIB),
    )(back)
    size = lax.ppermute(size, ("tm", "gx", "gy"), turned())
    new_modes = call(final_kernel, [(16, 64, 256)], 4, 0)(back, other, both, coef)[0]
    size, new_modes = lax.optimization_barrier((size, new_modes))
    return (new_field.reshape(1, 8, 8, 256), new_modes.reshape(1, 16, 8, 8, 256), size)


def solution(mesh):
    return jax.shard_map(
        per_device,
        mesh=mesh,
        in_specs=(
            P("tm", "gx", "gy", None),
            P("tm", None, "gx", "gy", None),
            P("gx", "gy", None),
            P("gx", "gy", None),
            P(),
            P(),
            P(),
        ),
        out_specs=(P("tm", "gx", "gy", None), P("tm", None, "gx", "gy", None), P("tm")),
        check_vma=False,
    )
```
